32 devices in a mesh: region: 4 (over y, x), shard: 8 (over z, core).
Axes of the slice: x: 2, y: 2, z: 4, core: 2. Of those that a mesh axis runs over, the one named last changes fastest.
Arguments:
- tiles: bfloat16 [32768, 512], P(('region', 'shard')), may hold values from -6 to 6
- tile_block: int32 [32768], P(('region', 'shard')), may hold values from 0 to 15
- neighbors: int32 [512, 64], P(('region', 'shard')), may hold values from 0 to 511, as said below
- counts: int32 [512], P(('region', 'shard')), may hold values from 1 to 64, as said below
- flows: int32 [512, 64], P(('region', 'shard')), may hold values from 0 to 22, as said below
- w_anchor: bfloat16 [512, 1024], P('shard'), may hold values from -0.25 to 0.25
- w_dest: bfloat16 [512, 1024], P('shard'), may hold values from -0.25 to 0.25
- w_hidden: bfloat16 [1024, 1024], P('shard'), may hold values from -0.1875 to 0.1875
- w_out: bfloat16 [1024], replicated, may hold values from -0.1875 to 0.1875
Outputs:
- hidden_grad: float32 [1024, 1024], P('shard')
- out_grad: float32 [1024], replicated
- loss: float32 [], replicated
The draws below stay inside these ranges and needn't reach their ends.
Inputs may be any that keep to these rules, and one draw needn't show every extreme that they name: `neighbors`: every destination lies in the anchor's region, at most 32 blocks from the anchor in the region's order; the first counts slots hold distinct blocks, the others hold the anchor itself. `counts`: some anchor of every region has all 64 slots valid. `flows`: zero in slots at or beyond the anchor's count; the first slot holds at least one trip.
All inputs are finite; a program needn't handle non-finite values.
Results may differ from the reference program's by a relative error of at most 0.017.
Values may be sent and summed in bfloat16 or wider, within the bound.
No kernel may reach another device: no remote copies, remote signals or barrier semaphores. Data moves between devices by JAX's collectives and lax.ppermute only.
A program may use at most 64 MiB of HBM per device.

```python
import jax
import jax.numpy as jnp
from jax import lax

D = 512
HID = 1024
NB = 64
BLK_DEV = 16
TILE_DEV = 1024
BLOCKS = 512
TILES = 32768
N_REGION = 4
N_SHARD = 8


def neighbor_plan(key):
    reach = 2 * BLK_DEV
    width = 2 * reach + 1
    region_size = BLK_DEV * N_SHARD
    blocks = jnp.arange(BLOCKS, dtype=jnp.int32)
    local = blocks % region_size
    device = blocks // BLK_DEV
    offsets = jnp.arange(width, dtype=jnp.int32) - reach
    candidate = local[:, None] + offsets[None, :]
    inside = (candidate >= 0) & (candidate < region_size)
    available = jnp.sum(inside.astype(jnp.int32), axis=1)
    key_dense, key_count, key_order, key_flow = jax.random.split(key, 4)
    density = jax.random.randint(key_dense, (N_REGION * N_SHARD,), 1, 5)[device]
    draws = jax.random.randint(key_count, (BLOCKS,), 1, NB // 4 + 1)
    chosen_count = jnp.minimum(draws * density, available)
    chosen_count = jnp.where(local == region_size // 2, NB, chosen_count)
    chosen_count = jnp.maximum(chosen_count, 1).astype(jnp.int32)
    priority = jax.random.randint(key_order, (BLOCKS, width), 0, 2 ** 20) * width + jnp.arange(width, dtype=jnp.int32)[None, :]
    priority = jnp.where(inside, priority, 2 ** 30 + jnp.arange(width, dtype=jnp.int32)[None, :])
    order = jnp.argsort(priority, axis=1, stable=True)[:, :NB]
    picked = jnp.take_along_axis(candidate, order, axis=1)
    slot = jnp.arange(NB, dtype=jnp.int32)[None, :]
    live = slot < chosen_count[:, None]
    dest = jnp.where(live, blocks[:, None] - local[:, None] + picked, blocks[:, None]).astype(jnp.int32)
    factor = 1 + 3 * blocks // BLOCKS
    trips = jax.random.randint(key_flow, (BLOCKS, NB), 0, 8) * factor[:, None]
    trips = jnp.where((blocks[:, None] == BLOCKS - 1) & (slot == 0), 7 * factor[:, None], trips)
    trips = jnp.where(live, trips, 0)
    trips = trips + jnp.where(slot == 0, 1, 0)
    return (dest, chosen_count, trips.astype(jnp.int32))


def draw_neighbors(key, part):
    return neighbor_plan(key)[0]


def draw_counts(key, part):
    return neighbor_plan(key)[1]


def draw_flows(key, part):
    return neighbor_plan(key)[2]


def place_ends(drawn, key, least, top_value):
    extent = drawn.shape
    place = [jax.random.randint(jax.random.fold_in(key, axis), (), 0, extent[axis]) for axis in range(len(extent))]
    drawn = drawn.at[tuple(place)].set(least)
    longest = extent.index(max(extent))
    place[longest] = (place[longest] + 1) % extent[longest]
    return drawn.at[tuple(place)].set(top_value)


def level_of(key, dims, pieces, low, high):
    def one(position, parts):
        steps = jax.random.uniform(jax.random.fold_in(jax.random.fold_in(key, 6), position), (parts,), jnp.float32, low / len(pieces), high / len(pieces))
        return jnp.repeat(jnp.exp(steps), dims[position] // parts).reshape((-1,) + (1,) * (len(dims) - position - 1))

    loudness = one(*pieces[0])
    for cut in pieces[1:]:
        loudness = loudness * one(*cut)
    return loudness


def bell_draw(own_key, shape, deviation, most, shards=(), kind=jnp.bfloat16):
    entries = jax.random.normal(own_key, shape, jnp.float32) * deviation
    if len(shards) > 0:
        entries = level_of(own_key, shape, shards, -0.22, 0.18) * entries
    return jnp.clip(entries, min=-most, max=most).astype(kind)


def setup_inputs(seed: int = 0) -> dict:
    key_list = jax.random.split(jax.random.key(seed), 10)
    return {
        "tiles": bell_draw(key_list[0], (TILES, D), 1.0, 6.0, ((0, 32),)),
        "tile_block": place_ends(jax.random.randint(key_list[1], (TILES,), 0, BLK_DEV), jax.random.fold_in(key_list[1], 1), 0, BLK_DEV - 1).astype(jnp.int32),
        "neighbors": draw_neighbors(jax.random.fold_in(key_list[9], 71), 0),
        "counts": draw_counts(jax.random.fold_in(key_list[9], 71), 0),
        "flows": draw_flows(jax.random.fold_in(key_list[9], 71), 0),
        "w_anchor": bell_draw(key_list[5], (D, HID), D ** -0.5, 0.25, ((0, 8),)),
        "w_dest": bell_draw(key_list[6], (D, HID), D ** -0.5, 0.25, ((0, 8),)),
        "w_hidden": bell_draw(key_list[7], (HID, HID), HID ** -0.5, 0.1875, ((0, 8),)),
        "w_out": bell_draw(key_list[8], (HID,), HID ** -0.5, 0.1875),
    }


def reference(tiles, tile_block, neighbors, counts, flows, w_anchor, w_dest, w_hidden, w_out):
    owner = jnp.arange(TILES, dtype=jnp.int32) // TILE_DEV * BLK_DEV + tile_block
    sums = jax.ops.segment_sum(tiles.astype(jnp.float32), owner, num_segments=BLOCKS)
    scale = lax.rsqrt(lax.optimization_barrier(jnp.mean(sums * sums, axis=-1, keepdims=True)) + 1e-05)
    features = (sums * scale).astype(jnp.bfloat16)
    anchor_proj = jnp.dot(features, w_anchor, preferred_element_type=jnp.float32)
    dest_proj = jnp.dot(features, w_dest, preferred_element_type=jnp.float32)
    valid = jnp.arange(NB, dtype=jnp.int32)[None, :] < counts[:, None]
    flow_f = flows.astype(jnp.float32)
    total = jnp.sum(flow_f)
    weight_out = w_out.astype(jnp.float32)
    steps = BLOCKS // BLK_DEV
    inputs = (anchor_proj.reshape(steps, BLK_DEV, HID), neighbors.reshape(steps, BLK_DEV, NB), valid.reshape(steps, BLK_DEV, NB), flow_f.reshape(steps, BLK_DEV, NB))

    def visit(carry, item):
        grad, gout, numer = carry
        anchor_part, dest_ids, mask, flow_part = item
        first = jnp.maximum(anchor_part[:, None, :] + dest_proj[dest_ids], 0.0).astype(jnp.bfloat16)
        first = first.reshape(BLK_DEV * NB, HID)
        second = jnp.dot(first, w_hidden, preferred_element_type=jnp.float32)
        active = jnp.maximum(second, 0.0)
        scores = lax.optimization_barrier(jnp.sum(active * weight_out, axis=-1)).reshape(BLK_DEV, NB)
        masked = jnp.where(mask, scores, -jnp.inf)
        top = lax.optimization_barrier(jnp.max(masked, axis=-1, keepdims=True))
        expo = jnp.where(mask, jnp.exp(scores - top), 0.0)
        mass = lax.optimization_barrier(jnp.sum(expo, axis=-1, keepdims=True))
        probs = expo / mass
        logp = scores - top - jnp.log(mass)
        anchor_total = lax.optimization_barrier(jnp.sum(flow_part, axis=-1, keepdims=True))
        sgrad = jnp.where(mask, probs * anchor_total - flow_part, 0.0) / total
        sgrad = sgrad.reshape(BLK_DEV * NB)
        pre = (sgrad[:, None] * weight_out * (second > 0)).astype(jnp.bfloat16)
        grad = grad + jnp.dot(first.T, pre, preferred_element_type=jnp.float32)
        gout = gout + lax.optimization_barrier(jnp.sum(sgrad[:, None] * active, axis=0))
        numer = numer - jnp.sum(jnp.where(mask, flow_part * logp, 0.0))
        return ((grad, gout, numer), None)
    start = (jnp.zeros((HID, HID), jnp.float32), jnp.zeros((HID,), jnp.float32), jnp.zeros((), jnp.float32))
    (grad, gout, numer), unused = lax.scan(visit, start, inputs)
    return (grad, gout, numer / total)
```

```python
import functools

import jax
import jax.numpy as jnp
from jax import lax
from jax.experimental import pallas as pl
from jax.experimental.pallas import tpu as pltpu
from jax.sharding import PartitionSpec as P

BF = jnp.bfloat16
F32 = jnp.float32
REACH = 2
TAIL = 16
MIB = 1024 * 1024
VMEM = pl.BlockSpec(memory_space=pltpu.VMEM)


def along_z(array, by):
    devices = lax.axis_size("shard")
    return lax.ppermute(array, "shard", [(i, (i + 2 * by) % devices) for i in range(devices)])


def swap_core(array):
    devices = lax.axis_size("shard")
    return lax.ppermute(array, "shard", [(i, i ^ 1) for i in range(devices)])


def swap_region(array, by):
    devices = lax.axis_size("region")
    return lax.ppermute(array, "region", [(i, i ^ by) for i in range(devices)])


def room(mib):
    return pltpu.CompilerParams(vmem_limit_bytes=int(mib * MIB))


def identity(n):
    same = lax.broadcasted_iota(jnp.int32, (n, n), 0) == lax.broadcasted_iota(jnp.int32, (n, n), 1)
    return jnp.where(same, 1.0, 0.0).astype(BF)


def turned(one, array):
    return lax.dot_general(one, array, (((1,), (1,)), ((), ())), preferred_element_type=F32).astype(BF)


def split(value):
    high = value.astype(BF)
    return high, (value - high.astype(F32)).astype(BF)


def pack_tail(sums):
    high, low = split(sums)
    return jnp.concatenate([high.astype(F32), low.astype(F32)], axis=0).astype(BF)


def unpack_tail(rows):
    wide = rows.astype(F32)
    return wide[:8] + wide[8:]


def unit_rows(shard_at, rows, cols, region):
    first = shard_at * rows
    return pl.ds(pl.multiple_of(((first // cols) ^ region) * cols + first % cols, rows), rows)


def score_kernel(n_region, n_z, blk, slots, *refs):
    half = 2 + n_region
    mine, other, rest = refs[:half], refs[half : 2 * half], refs[2 * half :]
    w_out, first_out, act_out, score_out, ids, flows, feat, own, w_in, w_mid, w_mid_t, table, tables, plain = rest
    step = pl.program_id(0)
    region = lax.axis_index("region")
    shard = lax.axis_index("shard")
    z, core = shard // 2, shard % 2
    window = (2 * REACH + 1) * blk
    lines = blk * slots // 128
    hidden, cols = w_mid.shape
    parts = feat.shape[1] // cols

    @pl.when(step == 0)
    def assemble():
        raw_cut = mine[0].shape[1] // 2
        dest_rows = (n_z - 1) * raw_cut
        feat_rows = 3 * parts * blk
        slot_row = dest_rows + feat_rows
        slot_rows = blk if cols >= 2 * slots else 2 * blk
        anchor_base = slot_row + slot_rows
        for source, core_at in ((mine, core), (other, 1 - core)):
            raw, mids, planes = source[0], source[1], source[2:]
            rows_mid = hidden // (2 * n_z)
            for j in range(n_z):
                shard_at = 2 * lax.rem(z - j + n_z, n_z) + core_at
                at = pl.ds(pl.multiple_of(shard_at * raw_cut, raw_cut), raw_cut)
                mid = rows_mid + (j - 1) * (rows_mid + raw_cut) if j > 0 else 0
                w_mid[unit_rows(shard_at, rows_mid, cols, region), :] = mids[mid : mid + rows_mid, :]
                for i in range(n_region):
                    base = (j - 1) * raw_cut
                    if j == 0:
                        w_in[i, at, :cols] = raw[i, :raw_cut, :]
                        w_in[i, at, cols:] = raw[i, raw_cut:, :]
                    else:
                        if i == n_region - 1:
                            w_in[i, at, :cols] = mids[mid + rows_mid : mid + rows_mid + raw_cut, :]
                        else:
                            w_in[i, at, :cols] = planes[i][anchor_base + base : anchor_base + base + raw_cut, :]
                        w_in[i, at, cols:] = planes[i][base : base + raw_cut, :]
        one = identity(cols)
        w_mid_t[...] = turned(one, w_mid[...])
        left = lax.broadcasted_iota(jnp.int32, (lines, 128), 1) < slots
        for i in range(n_region):
            near, far = mine[2 + i], other[2 + i]
            for t in range(parts):
                below, here, above = (
                    slice(dest_rows + (k * parts + t) * blk, dest_rows + (k * parts + t + 1) * blk) for k in range(3)
                )
                lanes = slice(t * cols, (t + 1) * cols)
                before = jnp.where(core == 0, far[below, :], far[here, :])
                after = jnp.where(core == 0, far[here, :], far[above, :])
                for k, part in enumerate((near[below, :], before, near[here, :], after, near[above, :])):
                    feat[i * window + k * blk : i * window + (k + 1) * blk, lanes] = part
                own[i * blk : (i + 1) * blk, lanes] = near[here, :]
            if slot_rows == blk:
                plain[...] = near[slot_row : slot_row + blk, : 2 * slots].astype(F32)
            else:
                plain[:, :slots] = near[slot_row : slot_row + blk, :slots].astype(F32)
                plain[:, slots:] = near[slot_row + blk : slot_row + 2 * blk, :slots].astype(F32)
            even = plain[pl.ds(0, lines, stride=2), :]
            odd = plain[pl.ds(1, lines, stride=2), :]
            ids[i] = jnp.where(left, even, pltpu.roll(odd, slots, 1))
            flows[i] = jnp.where(left, pltpu.roll(even, slots, 1), odd)
        for k in range(n_region):
            lanes = slice(k * cols, (k + 1) * cols)
            high, low = split(jnp.dot(feat[...], w_in[k, :, cols:], preferred_element_type=F32))
            high_a, low_a = split(jnp.dot(own[...], w_in[k, :, :cols], preferred_element_type=F32))
            for i in range(n_region):
                table[i, :window, lanes] = high[i * window : (i + 1) * window]
                table[i, window : 2 * window, lanes] = low[i * window : (i + 1) * window]
                table[i, 2 * window : 2 * window + blk, lanes] = high_a[i * blk : (i + 1) * blk]
                table[i, 2 * window + blk :, lanes] = low_a[i * blk : (i + 1) * blk]
        wide = one if cols == 256 else identity(256)
        for i in range(n_region):
            for k in range(0, hidden, 256):
                tables[i, k : k + 256, :] = turned(wide, table[i, :, k : k + 256])

    group = 8
    pairs = group * slots
    spread = pairs // 128
    chosen = ids[step]
    lookup = tables[step]
    dest_row = lax.broadcasted_iota(jnp.int32, (2 * window, pairs), 0)
    dest_row = jnp.where(dest_row >= window, dest_row - window, dest_row).astype(F32)
    anchor_row = lax.broadcasted_iota(jnp.int32, (2 * blk, pairs), 0)
    anchor_row = jnp.where(anchor_row >= blk, anchor_row - blk, anchor_row)
    anchor_lane = lax.broadcasted_iota(jnp.int32, (2 * blk, pairs), 1) // slots
    weight = w_out[...]
    for c in range(blk // group):
        at = slice(c * pairs, (c + 1) * pairs)
        spot = jnp.concatenate([chosen[c * spread + k : c * spread + k + 1, :] for k in range(spread)], axis=1)
        dest_hot = jnp.where(dest_row == spot, 1.0, 0.0)
        anchor_hot = jnp.where(anchor_row == anchor_lane + c * group, 1.0, 0.0)
        onehot = jnp.concatenate([dest_hot, anchor_hot], axis=0).astype(BF)
        first = jnp.maximum(jnp.dot(lookup, onehot, preferred_element_type=F32).astype(BF), 0)
        first_out[:, at] = first
        active = jnp.maximum(jnp.dot(w_mid_t[...], first, preferred_element_type=F32), 0.0)
        act_out[:, at] = active.astype(BF)
        score = jnp.sum(active * weight, axis=0, keepdims=True)
        for k in range(spread):
            score_out[c * spread + k : c * spread + k + 1, :] = score[:, k * 128 : (k + 1) * 128]


def grad_kernel(n_region, n_z, slots, *refs):
    scores, rest = refs[:n_region], refs[n_region:]
    ids, flows, first, act, w_out, keep, send, grad, gout, sums = rest
    step = pl.program_id(0)
    cols = act.shape[0]

    @pl.when(step == 0)
    def clear():
        grad[...] = jnp.zeros_like(grad)
        gout[...] = jnp.zeros_like(gout)
        sums[...] = jnp.zeros_like(sums)

    score = scores[0][...]
    for other in scores[1:]:
        score = score + other[...]
    valid = ids[step] >= 0
    left = lax.broadcasted_iota(jnp.int32, score.shape, 1) < slots

    def halves(reduce, value, rest):
        low = reduce(jnp.where(left, value, rest), axis=1, keepdims=True)
        high = reduce(jnp.where(left, rest, value), axis=1, keepdims=True)
        return jnp.where(left, low, high)

    top = halves(jnp.max, jnp.where(valid, score, -jnp.inf), -jnp.inf)
    expo = jnp.where(valid, jnp.exp(score - top), 0.0)
    mass = halves(jnp.sum, expo, 0.0)
    probs = expo / mass
    logp = score - top - jnp.log(mass)
    flow = flows[step]
    anchor_total = halves(jnp.sum, flow, 0.0)
    sgrad = jnp.where(valid, probs * anchor_total - flow, 0.0)
    sums[0] += flow
    sums[1] -= jnp.where(valid, flow * logp, 0.0)

    lanes = score.shape[1]
    weight = jnp.broadcast_to(w_out[...], (cols, lanes))
    pre = []
    for q in range(score.shape[0]):
        line = sgrad[q : q + 1, :]
        active = act[:, q * lanes : (q + 1) * lanes].astype(F32)
        gained = active * line if q == 0 else gained + active * line
        pre.append(jnp.where(active > 0, weight * line, 0.0).astype(BF))
    gout[...] += gained
    pre = jnp.concatenate(pre, axis=1)
    grad[...] += lax.dot_general(first[...], pre, (((1,), (1,)), ((), ())), preferred_element_type=F32)

    @pl.when(step == n_region - 1)
    def finish():
        out = jnp.sum(gout[...].T, axis=0, keepdims=True)
        total = jnp.sum(sums[0])
        numer = jnp.sum(sums[1])
        row = lax.broadcasted_iota(jnp.int32, (8, cols), 0)
        lane = lax.broadcasted_iota(jnp.int32, (8, cols), 1)
        stats = jnp.where(lane == 0, total, jnp.where(lane == 1, numer, 0.0))
        tail = pack_tail(jnp.where(row == 0, out, jnp.where(row == 1, stats, 0.0)))
        rows = keep.shape[1] - TAIL
        region = lax.axis_index("region")
        shard = lax.axis_index("shard")
        z, core = shard // 2, shard % 2
        for j in range(n_z):
            z_at = lax.rem(z + j, n_z)
            for target, core_at in ((keep, core), (send, 1 - core)):
                target[j, :rows, :] = grad[unit_rows(2 * z_at + core_at, rows, cols, region), :].astype(BF)
                target[j, rows:, :] = tail


def core_sum_kernel(keep, received, *outs):
    for j, out in enumerate(outs):
        rows = out.shape[0] - TAIL
        out[:rows, :] = (keep[j, :rows, :].astype(F32) + received[j, :rows, :].astype(F32)).astype(BF)
        out[rows:, :] = pack_tail(unpack_tail(keep[j, rows:, :]) + unpack_tail(received[j, rows:, :]))


def z_sum_kernel(*refs):
    blocks, (out, tails) = refs[:-2], refs[-2:]
    n_z = len(blocks)
    rows = out.shape[0] - TAIL
    total = blocks[0][:rows, :].astype(F32)
    for block in blocks[1:]:
        total = total + block[:rows, :].astype(F32)
    out[:rows, :] = total.astype(BF)
    for j, block in enumerate(blocks):
        tails[j] = unpack_tail(block[rows:, :])
    z = lax.axis_index("shard") // 2
    tail = tails[z]
    for z_at in range(1, n_z):
        tail = tail + tails[lax.rem(z - z_at + n_z, n_z)]
    out[rows:, :] = pack_tail(tail)


def finish_kernel(*refs):
    blocks, (grad, out_grad, loss, held) = refs[:-4], refs[-4:]
    n_region = len(blocks)
    cols = blocks[0].shape[1]
    rows = grad.shape[0]
    for i, block in enumerate(blocks):
        held[i] = block[...]
    region = lax.axis_index("region")
    stats = unpack_tail(held[region][rows:, :])
    total = stats[1:2, 0:1]
    numer = stats[1:2, 1:2]
    loss[...] = numer / total
    inverse = 1.0 / total
    for q in range(n_region):
        block = held[region ^ q]
        grad[:, q * cols : (q + 1) * cols] = block[:rows, :].astype(F32) * inverse
        out_grad[:, q * cols : (q + 1) * cols] = unpack_tail(block[rows:, :])[0:1, :] * inverse


def shards(tiles, tile_block, neighbors, counts, flows, w_anchor, w_dest, w_hidden, w_out):
    blk = counts.shape[0]
    slots = neighbors.shape[1]
    n_region = lax.axis_size("region")
    n_shard = lax.axis_size("shard")
    n_z = n_shard // 2
    hidden = w_hidden.shape[1]
    rows_in = w_anchor.shape[0]
    depth = rows_in * n_shard
    cols = hidden // n_region
    pairs = blk * slots
    lines = pairs // 128
    window = (2 * REACH + 1) * blk
    region = lax.axis_index("region")

    def cut(array, i):
        return lax.dynamic_slice_in_dim(array, (region ^ i) * cols, cols, array.ndim - 1)

    def along_rows(features):
        return [features[:, t * cols : (t + 1) * cols] for t in range(depth // cols)]

    raw = jnp.stack([jnp.concatenate([cut(w_anchor, i), cut(w_dest, i)], axis=0) for i in range(n_region)])
    piece = jnp.concatenate([cut(w_anchor, 0), cut(w_dest, 0)], axis=0)

    piece, tile_block = lax.optimization_barrier((piece, tile_block))
    onehot = (tile_block[None, :] == jnp.arange(blk, dtype=jnp.int32)[:, None]).astype(BF)
    sums = jnp.dot(onehot, tiles, preferred_element_type=F32)
    scale = lax.rsqrt(jnp.mean(sums * sums, axis=-1, keepdims=True) + 1e-05)
    features = jnp.concatenate(along_rows((sums * scale).astype(BF)), axis=0)

    payload = jnp.concatenate([piece, features], axis=0)
    from_z = [along_z(payload if j in (1, n_z - 1) else piece, j) for j in range(1, n_z)]

    spot = neighbors % (blk * n_shard) - (lax.axis_index("shard") - REACH) * blk
    valid = jnp.arange(slots, dtype=jnp.int32)[None, :] < counts[:, None]
    slot_table = jnp.concatenate([jnp.where(valid, spot, -1), flows], axis=1 if cols >= 2 * slots else 0).astype(BF)
    slot_table = jnp.pad(slot_table, ((0, 0), (0, cols - slot_table.shape[1])))

    held = 2 * rows_in
    ends = [p[held:] for p in (from_z[0], from_z[-1])]
    shared = jnp.concatenate([p[rows_in:held] for p in from_z] + [ends[0], features, ends[1], slot_table], axis=0)
    plane = jnp.concatenate([shared] + [p[:rows_in] for p in from_z], axis=0)
    planes = [plane] + [swap_region(plane, i) for i in range(1, n_region - 1)] + [swap_region(shared, n_region - 1)]

    mid_raw = cut(w_hidden, 0)
    far_plane = swap_core(plane)
    mid_send, far_plane = lax.optimization_barrier(
        (jnp.concatenate([mid_raw, cut(w_anchor, n_region - 1)], axis=0), far_plane)
    )
    mids = jnp.concatenate([mid_raw] + [along_z(mid_send, j) for j in range(1, n_z)], axis=0)
    mine = [raw, mids, *planes]
    other = [swap_core(raw), swap_core(mids), far_plane] + [swap_core(x) for x in planes[1:]]
    weight_out = cut(w_out, 0).astype(F32).reshape(cols, 1)

    first, act, score, ids, flow = pl.pallas_call(
        functools.partial(score_kernel, n_region, n_z, blk, slots),
        grid=(n_region,),
        in_specs=[VMEM] * (2 * len(mine) + 1),
        out_specs=[
            pl.BlockSpec((hidden, pairs), lambda i: (0, i)),
            pl.BlockSpec((cols, pairs), lambda i: (0, i)),
            pl.BlockSpec((lines, 128), lambda i: (i, 0)),
            VMEM,
            VMEM,
        ],
        scratch_shapes=[
            pltpu.VMEM((n_region * window, depth), BF),
            pltpu.VMEM((n_region * blk, depth), BF),
            pltpu.VMEM((n_region, depth, 2 * cols), BF),
            pltpu.VMEM((hidden, cols), BF),
            pltpu.VMEM((cols, hidden), BF),
            pltpu.VMEM((n_region, 2 * (window + blk), hidden), BF),
            pltpu.VMEM((n_region, hidden, 2 * (window + blk)), BF),
            pltpu.VMEM((blk, 2 * slots), F32),
        ],
        out_shape=[
            jax.ShapeDtypeStruct((hidden, n_region * pairs), BF),
            jax.ShapeDtypeStruct((cols, n_region * pairs), BF),
            jax.ShapeDtypeStruct((n_region * lines, 128), F32),
            jax.ShapeDtypeStruct((n_region, lines, 128), F32),
            jax.ShapeDtypeStruct((n_region, lines, 128), F32),
        ],
        compiler_params=room(14 + 1.25 * n_region),
        name="scores",
    )(*mine, *other, weight_out)

    parts = [score] + [swap_region(score, i) for i in range(1, n_region)]
    rows = hidden // n_shard
    block = jax.ShapeDtypeStruct((rows + TAIL, cols), BF)
    blocks = jax.ShapeDtypeStruct((n_z, rows + TAIL, cols), BF)
    keep, send = pl.pallas_call(
        functools.partial(grad_kernel, n_region, n_z, slots),
        grid=(n_region,),
        in_specs=[pl.BlockSpec((lines, 128), functools.partial(lambda k, i: (i ^ k, 0), k)) for k in range(n_region)]
        + [
            VMEM,
            VMEM,
            pl.BlockSpec((hidden, pairs), lambda i: (0, i)),
            pl.BlockSpec((cols, pairs), lambda i: (0, i)),
            VMEM,
        ],
        out_specs=[VMEM, VMEM],
        scratch_shapes=[
            pltpu.VMEM((hidden, cols), F32),
            pltpu.VMEM((cols, 128), F32),
            pltpu.VMEM((2, lines, 128), F32),
        ],
        out_shape=[blocks, blocks],
        compiler_params=room(14),
        name="gradient",
    )(*parts, ids, flow, first, act, weight_out)

    own_rows = pl.pallas_call(
        core_sum_kernel,
        in_specs=[VMEM] * 2,
        out_specs=[VMEM] * n_z,
        out_shape=[block] * n_z,
        compiler_params=room(4),
        name="core_sum",
    )(keep, swap_core(send))
    own_rows = [own_rows[0]] + [along_z(own_rows[j], j) for j in range(1, n_z)]
    reduced = pl.pallas_call(
        z_sum_kernel,
        in_specs=[VMEM] * n_z,
        out_specs=VMEM,
        out_shape=block,
        scratch_shapes=[pltpu.VMEM((n_z, 8, cols), F32)],
        compiler_params=room(4),
        name="z_sum",
    )(*own_rows)
    final = [reduced] + [swap_region(reduced, i) for i in range(1, n_region)]
    hidden_grad, out_grad, loss = pl.pallas_call(
        finish_kernel,
        in_specs=[VMEM] * n_region,
        out_specs=[VMEM] * 3,
        out_shape=[
            jax.ShapeDtypeStruct((rows, hidden), F32),
            jax.ShapeDtypeStruct((1, hidden), F32),
            jax.ShapeDtypeStruct((1, 1), F32),
        ],
        scratch_shapes=[pltpu.VMEM((n_region, rows + TAIL, cols), BF)],
        compiler_params=room(4),
        name="finish",
    )(*final)
    return (hidden_grad, out_grad.reshape(hidden), loss.reshape(()))


def solution(mesh):
    return jax.shard_map(
        shards,
        mesh=mesh,
        in_specs=(
            P(("region", "shard"), None),
            P(("region", "shard")),
            P(("region", "shard"), None),
            P(("region", "shard")),
            P(("region", "shard"), None),
            P("shard", None),
            P("shard", None),
            P("shard", None),
            P(),
        ),
        out_specs=(P("shard", None), P(), P()),
        check_vma=False,
    )
```

```python
import functools

import jax
import jax.numpy as jnp
from jax import lax
from jax.experimental import pallas as pl
from jax.experimental.pallas import tpu as pltpu
from jax.sharding import PartitionSpec as P

BF = jnp.bfloat16
F32 = jnp.float32
REACH = 2
TAIL = 16
MIB = 1024 * 1024
VMEM = pl.BlockSpec(memory_space=pltpu.VMEM)


def along_z(array, by):
    devices = lax.axis_size("shard")
    return lax.ppermute(array, "shard", [(i, i ^ (2 * by)) for i in range(devices)])


def next_steps(n_z):
    return [j for j in range(1, n_z) if j & (j + 1) == 0]


def swap_core(array):
    devices = lax.axis_size("shard")
    return lax.ppermute(array, "shard", [(i, i ^ 1) for i in range(devices)])


def swap_region(array, by):
    devices = lax.axis_size("region")
    return lax.ppermute(array, "region", [(i, i ^ by) for i in range(devices)])


def room(mib):
    return pltpu.CompilerParams(vmem_limit_bytes=int(mib * MIB))


def identity(n):
    same = lax.broadcasted_iota(jnp.int32, (n, n), 0) == lax.broadcasted_iota(jnp.int32, (n, n), 1)
    return jnp.where(same, 1.0, 0.0).astype(BF)


def turned(one, array):
    return lax.dot_general(one, array, (((1,), (1,)), ((), ())), preferred_element_type=F32).astype(BF)


def split(value):
    high = value.astype(BF)
    return high, (value - high.astype(F32)).astype(BF)


def pack_tail(sums):
    high, low = split(sums)
    return jnp.concatenate([high.astype(F32), low.astype(F32)], axis=0).astype(BF)


def unpack_tail(rows):
    wide = rows.astype(F32)
    return wide[:8] + wide[8:]


def unit_rows(shard_at, rows, cols, region):
    first = shard_at * rows
    return pl.ds(pl.multiple_of(((first // cols) ^ region) * cols + first % cols, rows), rows)


def score_kernel(n_region, n_z, blk, slots, *refs):
    half = 2 + n_region
    mine, other, rest = refs[:half], refs[half : 2 * half], refs[2 * half :]
    w_out, first_out, act_out, score_out, ids, flows, feat, own, w_in, w_mid, w_mid_t, table, tables, plain = rest
    step = pl.program_id(0)
    region = lax.axis_index("region")
    shard = lax.axis_index("shard")
    z, core = shard // 2, shard % 2
    window = (2 * REACH + 1) * blk
    lines = blk * slots // 128
    hidden, cols = w_mid.shape
    parts = feat.shape[1] // cols

    @pl.when(step == 0)
    def assemble():
        raw_cut = mine[0].shape[1] // 2
        dest_rows = (n_z - 1) * raw_cut
        steps = next_steps(n_z)
        feat_rows = (1 + len(steps)) * parts * blk
        slot_row = dest_rows + feat_rows
        slot_rows = blk if cols >= 2 * slots else 2 * blk
        anchor_base = slot_row + slot_rows
        for source, core_at in ((mine, core), (other, 1 - core)):
            raw, mids, planes = source[0], source[1], source[2:]
            rows_mid = hidden // (2 * n_z)
            for j in range(n_z):
                shard_at = 2 * (z ^ j) + core_at
                at = pl.ds(pl.multiple_of(shard_at * raw_cut, raw_cut), raw_cut)
                mid = rows_mid + (j - 1) * (rows_mid + raw_cut) if j > 0 else 0
                w_mid[unit_rows(shard_at, rows_mid, cols, region), :] = mids[mid : mid + rows_mid, :]
                for i in range(n_region):
                    base = (j - 1) * raw_cut
                    if j == 0:
                        w_in[i, at, :cols] = raw[i, :raw_cut, :]
                        w_in[i, at, cols:] = raw[i, raw_cut:, :]
                    else:
                        if i == n_region - 1:
                            w_in[i, at, :cols] = mids[mid + rows_mid : mid + rows_mid + raw_cut, :]
                        else:
                            w_in[i, at, :cols] = planes[i][anchor_base + base : anchor_base + base + raw_cut, :]
                        w_in[i, at, cols:] = planes[i][base : base + raw_cut, :]
        one = identity(cols)
        w_mid_t[...] = turned(one, w_mid[...])
        left = lax.broadcasted_iota(jnp.int32, (lines, 128), 1) < slots
        below_at = sum(jnp.where((z ^ (z - 1)) >= j, 1, 0) for j in steps)
        above_at = sum(jnp.where((z ^ (z + 1)) >= j, 1, 0) for j in steps)
        for i in range(n_region):
            near, far = mine[2 + i], other[2 + i]
            for t in range(parts):
                below, here, above = (
                    pl.ds(pl.multiple_of(dest_rows + (k * parts + t) * blk, blk), blk) for k in (below_at, 0, above_at)
                )
                lanes = slice(t * cols, (t + 1) * cols)
                before = jnp.where(core == 0, far[below, :], far[here, :])
                after = jnp.where(core == 0, far[here, :], far[above, :])
                for k, part in enumerate((near[below, :], before, near[here, :], after, near[above, :])):
                    feat[i * window + k * blk : i * window + (k + 1) * blk, lanes] = part
                own[i * blk : (i + 1) * blk, lanes] = near[here, :]
            if slot_rows == blk:
                plain[...] = near[slot_row : slot_row + blk, : 2 * slots].astype(F32)
            else:
                plain[:, :slots] = near[slot_row : slot_row + blk, :slots].astype(F32)
                plain[:, slots:] = near[slot_row + blk : slot_row + 2 * blk, :slots].astype(F32)
            even = plain[pl.ds(0, lines, stride=2), :]
            odd = plain[pl.ds(1, lines, stride=2), :]
            ids[i] = jnp.where(left, even, pltpu.roll(odd, slots, 1))
            flows[i] = jnp.where(left, pltpu.roll(even, slots, 1), odd)
        for k in range(n_region):
            lanes = slice(k * cols, (k + 1) * cols)
            high, low = split(jnp.dot(feat[...], w_in[k, :, cols:], preferred_element_type=F32))
            high_a, low_a = split(jnp.dot(own[...], w_in[k, :, :cols], preferred_element_type=F32))
            for i in range(n_region):
                table[i, :window, lanes] = high[i * window : (i + 1) * window]
                table[i, window : 2 * window, lanes] = low[i * window : (i + 1) * window]
                table[i, 2 * window : 2 * window + blk, lanes] = high_a[i * blk : (i + 1) * blk]
                table[i, 2 * window + blk :, lanes] = low_a[i * blk : (i + 1) * blk]
        wide = one if cols == 256 else identity(256)
        for i in range(n_region):
            for k in range(0, hidden, 256):
                tables[i, k : k + 256, :] = turned(wide, table[i, :, k : k + 256])

    group = 8
    pairs = group * slots
    spread = pairs // 128
    dest_row = lax.broadcasted_iota(jnp.int32, (2 * window, pairs), 0)
    dest_row = jnp.where(dest_row >= window, dest_row - window, dest_row).astype(F32)
    anchor_row = lax.broadcasted_iota(jnp.int32, (2 * blk, pairs), 0)
    anchor_row = jnp.where(anchor_row >= blk, anchor_row - blk, anchor_row)
    anchor_lane = lax.broadcasted_iota(jnp.int32, (2 * blk, pairs), 1) // slots
    weight = w_out[...]
    for n in range(first_out.shape[1] // (blk * slots)):
        chosen = ids[step + n]
        lookup = tables[step + n]
        for c in range(blk // group):
            spot = jnp.concatenate([chosen[c * spread + k : c * spread + k + 1, :] for k in range(spread)], axis=1)
            dest_hot = jnp.where(dest_row == spot, 1.0, 0.0)
            anchor_hot = jnp.where(anchor_row == anchor_lane + c * group, 1.0, 0.0)
            onehot = jnp.concatenate([dest_hot, anchor_hot], axis=0).astype(BF)
            first = jnp.maximum(jnp.dot(lookup, onehot, preferred_element_type=F32).astype(BF), 0)
            at = slice(n * blk * slots + c * pairs, n * blk * slots + (c + 1) * pairs)
            first_out[:, at] = first
            active = jnp.maximum(jnp.dot(w_mid_t[...], first, preferred_element_type=F32), 0.0)
            act_out[:, at] = active.astype(BF)
            score = jnp.sum(active * weight, axis=0, keepdims=True)
            for k in range(spread):
                row = n * lines + c * spread + k
                score_out[row : row + 1, :] = score[:, k * 128 : (k + 1) * 128]


def target_rows(first, targets, rows, cols):
    z = lax.axis_index("shard") // 2
    region = lax.axis_index("region")
    return jnp.concatenate(
        [first[unit_rows(z ^ j, 2 * rows, cols, region), :] for j in targets], axis=0
    )


def put_blocks(grad, tail, keep, send):
    rows = keep.shape[1] - TAIL
    core = lax.axis_index("shard") % 2
    for n in range(keep.shape[0]):
        for target, core_at in ((keep, core), (send, 1 - core)):
            at = pl.ds(pl.multiple_of((2 * n + core_at) * rows, rows), rows)
            target[n, :rows, :] = grad[at, :].astype(BF)
            target[n, rows:, :] = tail


def rest_kernel(targets, *refs):
    first, pre, tail, keep, send, grad = refs
    rows = keep.shape[1] - TAIL
    step = pl.program_id(0)
    part = lax.dot_general(
        target_rows(first, targets, rows, pre.shape[0]),
        pre[...],
        (((1,), (1,)), ((), ())),
        preferred_element_type=F32,
    )

    @pl.when(step == 0)
    def begin():
        grad[...] = part

    @pl.when(step > 0)
    def more():
        grad[...] += part

    @pl.when(step == pl.num_programs(0) - 1)
    def finish():
        put_blocks(grad, tail[...], keep, send)


def grad_kernel(n_region, targets, slots, *refs):
    scores, rest = refs[:n_region], refs[n_region:]
    ids, flows, first, act, w_out, pre_out, tail_out, keep, send, grad, gout, sums = rest
    step = pl.program_id(0)
    cols = act.shape[0]
    rows = keep.shape[1] - TAIL
    lines, lanes = ids.shape[1:]

    @pl.when(step == 0)
    def clear():
        grad[...] = jnp.zeros_like(grad)
        gout[...] = jnp.zeros_like(gout)
        sums[...] = jnp.zeros_like(sums)

    left = lax.broadcasted_iota(jnp.int32, (lines, lanes), 1) < slots

    def halves(reduce, value, rest):
        low = reduce(jnp.where(left, value, rest), axis=1, keepdims=True)
        high = reduce(jnp.where(left, rest, value), axis=1, keepdims=True)
        return jnp.where(left, low, high)

    weight = jnp.broadcast_to(w_out[...], (cols, lanes))
    gained = gout[...]
    trips, numer = sums[0], sums[1]
    for n in range(act.shape[1] // (lines * lanes)):
        score = scores[0][n * lines : (n + 1) * lines, :]
        for k in range(1, n_region):
            at = (n ^ k) * lines if scores[k].shape[0] > lines else 0
            score = score + scores[k][at : at + lines, :]
        valid = ids[step + n] >= 0
        top = halves(jnp.max, jnp.where(valid, score, -jnp.inf), -jnp.inf)
        expo = jnp.where(valid, jnp.exp(score - top), 0.0)
        mass = halves(jnp.sum, expo, 0.0)
        probs = expo / mass
        logp = score - top - jnp.log(mass)
        flow = flows[step + n]
        anchor_total = halves(jnp.sum, flow, 0.0)
        sgrad = jnp.where(valid, probs * anchor_total - flow, 0.0)
        trips = trips + flow
        numer = numer - jnp.where(valid, flow * logp, 0.0)
        for q in range(lines):
            line = sgrad[q : q + 1, :]
            at = slice((n * lines + q) * lanes, (n * lines + q + 1) * lanes)
            active = act[:, at].astype(F32)
            gained = gained + active * line
            pre_out[:, at] = jnp.where(active > 0, weight * line, 0.0).astype(BF)
    gout[...] = gained
    sums[0] = trips
    sums[1] = numer
    grad[...] += lax.dot_general(
        target_rows(first, targets, rows, cols), pre_out[...], (((1,), (1,)), ((), ())), preferred_element_type=F32
    )

    @pl.when(step == pl.num_programs(0) - 1)
    def finish():
        out = jnp.sum(gout[...].T, axis=0, keepdims=True)
        total = jnp.sum(sums[0])
        numer = jnp.sum(sums[1])
        row = lax.broadcasted_iota(jnp.int32, (8, cols), 0)
        lane = lax.broadcasted_iota(jnp.int32, (8, cols), 1)
        stats = jnp.where(lane == 0, total, jnp.where(lane == 1, numer, 0.0))
        tail = pack_tail(jnp.where(row == 0, out, jnp.where(row == 1, stats, 0.0)))
        tail_out[...] = tail
        put_blocks(grad, tail, keep, send)


def core_sum_kernel(keep, received, *outs):
    for j, out in enumerate(outs):
        rows = out.shape[0] - TAIL
        out[:rows, :] = (keep[j, :rows, :].astype(F32) + received[j, :rows, :].astype(F32)).astype(BF)
        out[rows:, :] = pack_tail(unpack_tail(keep[j, rows:, :]) + unpack_tail(received[j, rows:, :]))


def z_sum_kernel(steps, *refs):
    blocks, (out, tails) = refs[:-2], refs[-2:]
    n_z = len(blocks)
    rows = out.shape[0] - TAIL
    total = blocks[0][:rows, :].astype(F32)
    for block in blocks[1:]:
        total = total + block[:rows, :].astype(F32)
    out[:rows, :] = total.astype(BF)
    for j, block in zip(steps, blocks):
        tails[j] = unpack_tail(block[rows:, :])
    z = lax.axis_index("shard") // 2
    tail = tails[z]
    for z_at in range(1, n_z):
        tail = tail + tails[z ^ z_at]
    out[rows:, :] = pack_tail(tail)


def finish_kernel(*refs):
    blocks, (grad, out_grad, loss, held) = refs[:-4], refs[-4:]
    n_region = len(blocks)
    cols = blocks[0].shape[1]
    rows = grad.shape[0]
    for i, block in enumerate(blocks):
        held[i] = block[...]
    region = lax.axis_index("region")
    stats = unpack_tail(held[region][rows:, :])
    total = stats[1:2, 0:1]
    numer = stats[1:2, 1:2]
    loss[...] = numer / total
    inverse = 1.0 / total
    for q in range(n_region):
        block = held[region ^ q]
        grad[:, q * cols : (q + 1) * cols] = block[:rows, :].astype(F32) * inverse
        out_grad[:, q * cols : (q + 1) * cols] = unpack_tail(block[rows:, :])[0:1, :] * inverse


def shards(tiles, tile_block, neighbors, counts, flows, w_anchor, w_dest, w_hidden, w_out):
    blk = counts.shape[0]
    slots = neighbors.shape[1]
    n_region = lax.axis_size("region")
    n_shard = lax.axis_size("shard")
    n_z = n_shard // 2
    hidden = w_hidden.shape[1]
    rows_in = w_anchor.shape[0]
    depth = rows_in * n_shard
    cols = hidden // n_region
    pairs = blk * slots
    lines = pairs // 128
    window = (2 * REACH + 1) * blk
    region = lax.axis_index("region")

    def cut(array, i):
        return lax.dynamic_slice_in_dim(array, (region ^ i) * cols, cols, array.ndim - 1)

    def along_rows(features):
        return [features[:, t * cols : (t + 1) * cols] for t in range(depth // cols)]

    piece = jnp.concatenate([cut(w_anchor, 0), cut(w_dest, 0)], axis=0)

    last_cols = cut(w_anchor, n_region - 1)
    piece, tile_block = lax.optimization_barrier((piece, tile_block))
    onehot = (tile_block[None, :] == jnp.arange(blk, dtype=jnp.int32)[:, None]).astype(BF)
    sums = jnp.dot(onehot, tiles, preferred_element_type=F32)
    scale = lax.rsqrt(jnp.mean(sums * sums, axis=-1, keepdims=True) + 1e-05)
    features = jnp.concatenate(along_rows((sums * scale).astype(BF)), axis=0)

    payload = jnp.concatenate([piece, features], axis=0)
    from_z = [along_z(payload if j in next_steps(n_z) else piece, j) for j in range(1, n_z)]
    w_anchor, w_dest, w_out, w_hidden, payload = lax.optimization_barrier((w_anchor, w_dest, w_out, w_hidden, payload))
    raw = jnp.stack([jnp.concatenate([cut(w_anchor, i), cut(w_dest, i)], axis=0) for i in range(n_region)])
    weight_out = cut(w_out, 0).astype(F32).reshape(cols, 1)
    mid_raw = cut(w_hidden, 0)
    mid_send = jnp.concatenate([mid_raw, last_cols], axis=0)
    far_raw = swap_core(raw)
    far_raw, weight_out, mid_send, *from_z = lax.optimization_barrier((far_raw, weight_out, mid_send, *from_z))

    spot = neighbors % (blk * n_shard) - (lax.axis_index("shard") - REACH) * blk
    valid = jnp.arange(slots, dtype=jnp.int32)[None, :] < counts[:, None]
    slot_table = jnp.concatenate([jnp.where(valid, spot, -1), flows], axis=1 if cols >= 2 * slots else 0).astype(BF)
    slot_table = jnp.pad(slot_table, ((0, 0), (0, cols - slot_table.shape[1])))

    held = 2 * rows_in
    around = [features] + [from_z[j - 1][held:] for j in next_steps(n_z)]
    shared = jnp.concatenate([p[rows_in:held] for p in from_z] + around + [slot_table], axis=0)
    plane = jnp.concatenate([shared] + [p[:rows_in] for p in from_z], axis=0)
    far_plane = swap_core(plane)
    mid_send, far_plane = lax.optimization_barrier((mid_send, far_plane))
    planes = [swap_region(plane, i) for i in range(1, n_region - 1)] + [swap_region(shared, n_region - 1)]

    mids = [along_z(mid_send, j) for j in range(1, n_z - 1)]
    mid_send, mids[0] = lax.optimization_barrier((mid_send, mids[0]))
    mids.append(along_z(mid_send, n_z - 1))
    arrived = lax.optimization_barrier((*planes[::-1], *mids))
    planes, mids = arrived[: n_region - 1][::-1], arrived[n_region - 1 :]
    mids = jnp.concatenate([mid_raw, *mids], axis=0)
    mine = [raw, mids, plane, *planes]
    other = [far_raw, swap_core(mids), far_plane] + [swap_core(x) for x in planes]

    resident = 2 * hidden * n_region * pairs <= 12 * MIB

    steps = 1 if resident else n_region
    by_lines = VMEM if resident else pl.BlockSpec((lines, 128), lambda i: (i, 0))

    def by_pairs(rows):
        return VMEM if resident else pl.BlockSpec((rows, pairs), lambda i: (0, i))

    first, act, score, ids, flow = pl.pallas_call(
        functools.partial(score_kernel, n_region, n_z, blk, slots),
        grid=(steps,),
        in_specs=[VMEM] * (2 * len(mine) + 1),
        out_specs=[by_pairs(hidden), by_pairs(cols), by_lines, VMEM, VMEM],
        scratch_shapes=[
            pltpu.VMEM((n_region * window, depth), BF),
            pltpu.VMEM((n_region * blk, depth), BF),
            pltpu.VMEM((n_region, depth, 2 * cols), BF),
            pltpu.VMEM((hidden, cols), BF),
            pltpu.VMEM((cols, hidden), BF),
            pltpu.VMEM((n_region, 2 * (window + blk), hidden), BF),
            pltpu.VMEM((n_region, hidden, 2 * (window + blk)), BF),
            pltpu.VMEM((blk, 2 * slots), F32),
        ],
        out_shape=[
            jax.ShapeDtypeStruct((hidden, n_region * pairs), BF),
            jax.ShapeDtypeStruct((cols, n_region * pairs), BF),
            jax.ShapeDtypeStruct((n_region * lines, 128), F32),
            jax.ShapeDtypeStruct((n_region, lines, 128), F32),
            jax.ShapeDtypeStruct((n_region, lines, 128), F32),
        ],
        compiler_params=room(14 + 1.25 * n_region),
        name="scores",
    )(*mine, *other, weight_out)

    parts = [score] + [swap_region(score, i) for i in range(1, n_region)]
    rows = hidden // n_shard
    block = jax.ShapeDtypeStruct((rows + TAIL, cols), BF)
    order = list(range(n_z))[::-1]
    early, later, last = order[: n_z // 2], order[n_z // 2 : -1], order[-1:]

    def blocks(targets):
        return jax.ShapeDtypeStruct((len(targets), rows + TAIL, cols), BF)

    def core_sum(keep, received):
        return pl.pallas_call(
            core_sum_kernel,
            in_specs=[VMEM] * 2,
            out_specs=[VMEM] * keep.shape[0],
            out_shape=[block] * keep.shape[0],
            compiler_params=room(4),
            name="core_sum",
        )(keep, received)

    def rest(targets, pre):
        return pl.pallas_call(
            functools.partial(rest_kernel, targets),
            grid=(steps,),
            in_specs=[by_pairs(hidden), by_pairs(cols), VMEM],
            out_specs=[VMEM] * 2,
            scratch_shapes=[pltpu.VMEM((len(targets) * 2 * rows, cols), F32)],
            out_shape=[blocks(targets)] * 2,
            compiler_params=room(14),
            name="gradient_rest",
        )(first, pre, tail)

    pre, tail, keep, send = pl.pallas_call(
        functools.partial(grad_kernel, n_region, early, slots),
        grid=(steps,),
        in_specs=[
            VMEM if resident else pl.BlockSpec((lines, 128), functools.partial(lambda k, i: (i ^ k, 0), k))
            for k in range(n_region)
        ]
        + [VMEM, VMEM, by_pairs(hidden), by_pairs(cols), VMEM],
        out_specs=[by_pairs(cols)] + [VMEM] * 3,
        scratch_shapes=[
            pltpu.VMEM((len(early) * 2 * rows, cols), F32),
            pltpu.VMEM((cols, 128), F32),
            pltpu.VMEM((2, lines, 128), F32),
        ],
        out_shape=[
            jax.ShapeDtypeStruct((cols, n_region * pairs), BF),
            jax.ShapeDtypeStruct((TAIL, cols), BF),
            blocks(early),
            blocks(early),
        ],
        compiler_params=room(14),
        name="gradient",
    )(*parts, ids, flow, first, act, weight_out)
    received = swap_core(send)
    keep_later, send_later = rest(later, pre)
    sums = core_sum(keep, received)
    pre, *sums = lax.optimization_barrier((pre, *sums))
    received_later = swap_core(send_later)
    keep_last, send_last = rest(last, pre)
    received_last = swap_core(send_last)
    keep_later, received_later, keep_last = lax.optimization_barrier((keep_later, received_later, keep_last))
    sums = lax.optimization_barrier((*sums, *core_sum(keep_later, received_later)))
    arrived = [along_z(x, j) for x, j in zip(sums, early + later)]
    own_rows = [*core_sum(keep_last, received_last)] + arrived
    reduced = pl.pallas_call(
        functools.partial(z_sum_kernel, last + early + later),
        in_specs=[VMEM] * n_z,
        out_specs=VMEM,
        out_shape=block,
        scratch_shapes=[pltpu.VMEM((n_z, 8, cols), F32)],
        compiler_params=room(4),
        name="z_sum",
    )(*own_rows)
    final = [reduced] + [swap_region(reduced, i) for i in range(1, n_region)]
    hidden_grad, out_grad, loss = pl.pallas_call(
        finish_kernel,
        in_specs=[VMEM] * n_region,
        out_specs=[VMEM] * 3,
        out_shape=[
            jax.ShapeDtypeStruct((rows, hidden), F32),
            jax.ShapeDtypeStruct((1, hidden), F32),
            jax.ShapeDtypeStruct((1, 1), F32),
        ],
        scratch_shapes=[pltpu.VMEM((n_region, rows + TAIL, cols), BF)],
        compiler_params=room(4),
        name="finish",
    )(*final)
    return (hidden_grad, out_grad.reshape(hidden), loss.reshape(()))


def solution(mesh):
    return jax.shard_map(
        shards,
        mesh=mesh,
        in_specs=(
            P(("region", "shard"), None),
            P(("region", "shard")),
            P(("region", "shard"), None),
            P(("region", "shard")),
            P(("region", "shard"), None),
            P("shard", None),
            P("shard", None),
            P("shard", None),
            P(),
        ),
        out_specs=(P("shard", None), P(), P()),
        check_vma=False,
    )
```

```python
import functools

import jax
import jax.numpy as jnp
from jax import lax
from jax.experimental import pallas as pl
from jax.experimental.pallas import tpu as pltpu
from jax.sharding import PartitionSpec as P

BF = jnp.bfloat16
F32 = jnp.float32
REACH = 2
TAIL = 16
MIB = 1024 * 1024
VMEM = pl.BlockSpec(memory_space=pltpu.VMEM)


def along_z(array, by):
    devices = lax.axis_size("shard")
    return lax.ppermute(array, "shard", [(i, i ^ (2 * by)) for i in range(devices)])


def next_steps(n_z):
    return [j for j in range(1, n_z) if j & (j + 1) == 0]


def swap_core(array):
    devices = lax.axis_size("shard")
    return lax.ppermute(array, "shard", [(i, i ^ 1) for i in range(devices)])


def swap_region(array, by):
    devices = lax.axis_size("region")
    return lax.ppermute(array, "region", [(i, i ^ by) for i in range(devices)])


def room(mib):
    return pltpu.CompilerParams(vmem_limit_bytes=int(mib * MIB))


def identity(n):
    same = lax.broadcasted_iota(jnp.int32, (n, n), 0) == lax.broadcasted_iota(jnp.int32, (n, n), 1)
    return jnp.where(same, 1.0, 0.0).astype(BF)


def turned(one, array):
    return lax.dot_general(one, array, (((1,), (1,)), ((), ())), preferred_element_type=F32).astype(BF)


def split(value):
    high = value.astype(BF)
    return high, (value - high.astype(F32)).astype(BF)


def pack_tail(sums):
    high, low = split(sums)
    return jnp.concatenate([high.astype(F32), low.astype(F32)], axis=0).astype(BF)


def unpack_tail(rows):
    wide = rows.astype(F32)
    return wide[:8] + wide[8:]


def unit_rows(shard_at, rows, cols, region):
    first = shard_at * rows
    return pl.ds(pl.multiple_of(((first // cols) ^ region) * cols + first % cols, rows), rows)


def score_kernel(n_region, n_z, blk, slots, *refs):
    half = 2 + n_region
    mine, other, rest = refs[:half], refs[half : 2 * half], refs[2 * half :]
    w_out, first_out, act_out, score_out, ids, flows, feat, own, w_in, w_mid, w_mid_t, table, tables, plain = rest
    step = pl.program_id(0)
    region = lax.axis_index("region")
    shard = lax.axis_index("shard")
    z, core = shard // 2, shard % 2
    window = (2 * REACH + 1) * blk
    lines = blk * slots // 128
    hidden, cols = w_mid.shape
    parts = feat.shape[1] // cols

    @pl.when(step == 0)
    def assemble():
        raw_cut = mine[0].shape[1] // 2
        dest_rows = (n_z - 1) * raw_cut
        steps = next_steps(n_z)
        feat_rows = (1 + len(steps)) * parts * blk
        slot_row = dest_rows + feat_rows
        slot_rows = blk if cols >= 2 * slots else 2 * blk
        anchor_base = slot_row + slot_rows
        for source, core_at in ((mine, core), (other, 1 - core)):
            raw, mids, planes = source[0], source[1], source[2:]
            rows_mid = hidden // (2 * n_z)
            for j in range(n_z):
                shard_at = 2 * (z ^ j) + core_at
                at = pl.ds(pl.multiple_of(shard_at * raw_cut, raw_cut), raw_cut)
                mid = rows_mid + (n_z - 1 - j) * (rows_mid + raw_cut) if j > 0 else 0
                w_mid[unit_rows(shard_at, rows_mid, cols, region), :] = mids[mid : mid + rows_mid, :]
                for i in range(n_region):
                    base = (j - 1) * raw_cut
                    if j == 0:
                        w_in[i, at, :cols] = raw[i, :raw_cut, :]
                        w_in[i, at, cols:] = raw[i, raw_cut:, :]
                    else:
                        if i == n_region - 1:
                            w_in[i, at, :cols] = mids[mid + rows_mid : mid + rows_mid + raw_cut, :]
                        else:
                            w_in[i, at, :cols] = planes[i][anchor_base + base : anchor_base + base + raw_cut, :]
                        w_in[i, at, cols:] = planes[i][base : base + raw_cut, :]
        one = identity(cols)
        w_mid_t[...] = turned(one, w_mid[...])
        left = lax.broadcasted_iota(jnp.int32, (lines, 128), 1) < slots
        below_at = sum(jnp.where((z ^ (z - 1)) >= j, 1, 0) for j in steps)
        above_at = sum(jnp.where((z ^ (z + 1)) >= j, 1, 0) for j in steps)
        for i in range(n_region):
            near, far = mine[2 + i], other[2 + i]
            for t in range(parts):
                below, here, above = (
                    pl.ds(pl.multiple_of(dest_rows + (k * parts + t) * blk, blk), blk) for k in (below_at, 0, above_at)
                )
                lanes = slice(t * cols, (t + 1) * cols)
                before = jnp.where(core == 0, far[below, :], far[here, :])
                after = jnp.where(core == 0, far[here, :], far[above, :])
                for k, part in enumerate((near[below, :], before, near[here, :], after, near[above, :])):
                    feat[i * window + k * blk : i * window + (k + 1) * blk, lanes] = part
                own[i * blk : (i + 1) * blk, lanes] = near[here, :]
            if slot_rows == blk:
                plain[...] = near[slot_row : slot_row + blk, : 2 * slots].astype(F32)
            else:
                plain[:, :slots] = near[slot_row : slot_row + blk, :slots].astype(F32)
                plain[:, slots:] = near[slot_row + blk : slot_row + 2 * blk, :slots].astype(F32)
            even = plain[pl.ds(0, lines, stride=2), :]
            odd = plain[pl.ds(1, lines, stride=2), :]
            ids[i] = jnp.where(left, even, pltpu.roll(odd, slots, 1))
            flows[i] = jnp.where(left, pltpu.roll(even, slots, 1), odd)
        for k in range(n_region):
            lanes = slice(k * cols, (k + 1) * cols)
            high, low = split(jnp.dot(feat[...], w_in[k, :, cols:], preferred_element_type=F32))
            high_a, low_a = split(jnp.dot(own[...], w_in[k, :, :cols], preferred_element_type=F32))
            for i in range(n_region):
                table[i, :window, lanes] = high[i * window : (i + 1) * window]
                table[i, window : 2 * window, lanes] = low[i * window : (i + 1) * window]
                table[i, 2 * window : 2 * window + blk, lanes] = high_a[i * blk : (i + 1) * blk]
                table[i, 2 * window + blk :, lanes] = low_a[i * blk : (i + 1) * blk]
        wide = one if cols == 256 else identity(256)
        for i in range(n_region):
            for k in range(0, hidden, 256):
                tables[i, k : k + 256, :] = turned(wide, table[i, :, k : k + 256])

    group = 8
    pairs = group * slots
    spread = pairs // 128
    dest_row = lax.broadcasted_iota(jnp.int32, (2 * window, pairs), 0)
    dest_row = jnp.where(dest_row >= window, dest_row - window, dest_row).astype(F32)
    anchor_row = lax.broadcasted_iota(jnp.int32, (2 * blk, pairs), 0)
    anchor_row = jnp.where(anchor_row >= blk, anchor_row - blk, anchor_row)
    anchor_lane = lax.broadcasted_iota(jnp.int32, (2 * blk, pairs), 1) // slots
    weight = w_out[...]
    for n in range(first_out.shape[1] // (blk * slots)):
        chosen = ids[step + n]
        lookup = tables[step + n]
        for c in range(blk // group):
            spot = jnp.concatenate([chosen[c * spread + k : c * spread + k + 1, :] for k in range(spread)], axis=1)
            dest_hot = jnp.where(dest_row == spot, 1.0, 0.0)
            anchor_hot = jnp.where(anchor_row == anchor_lane + c * group, 1.0, 0.0)
            onehot = jnp.concatenate([dest_hot, anchor_hot], axis=0).astype(BF)
            first = jnp.maximum(jnp.dot(lookup, onehot, preferred_element_type=F32).astype(BF), 0)
            at = slice(n * blk * slots + c * pairs, n * blk * slots + (c + 1) * pairs)
            first_out[:, at] = first
            active = jnp.maximum(jnp.dot(w_mid_t[...], first, preferred_element_type=F32), 0.0)
            act_out[:, at] = active.astype(BF)
            score = jnp.sum(active * weight, axis=0, keepdims=True)
            for k in range(spread):
                row = n * lines + c * spread + k
                score_out[row : row + 1, :] = score[:, k * 128 : (k + 1) * 128]


def target_rows(first, targets, rows, cols):
    z = lax.axis_index("shard") // 2
    region = lax.axis_index("region")
    return jnp.concatenate(
        [first[unit_rows(z ^ j, 2 * rows, cols, region), :] for j in targets], axis=0
    )


def put_blocks(grad, tail, keep, send):
    rows = keep.shape[1] - TAIL
    core = lax.axis_index("shard") % 2
    for n in range(keep.shape[0]):
        for target, core_at in ((keep, core), (send, 1 - core)):
            at = pl.ds(pl.multiple_of((2 * n + core_at) * rows, rows), rows)
            target[n, :rows, :] = grad[at, :].astype(BF)
            target[n, rows:, :] = tail


def rest_kernel(targets, *refs):
    first, pre, tail, keep, send, grad = refs
    rows = keep.shape[1] - TAIL
    step = pl.program_id(0)
    part = lax.dot_general(
        target_rows(first, targets, rows, pre.shape[0]),
        pre[...],
        (((1,), (1,)), ((), ())),
        preferred_element_type=F32,
    )

    @pl.when(step == 0)
    def begin():
        grad[...] = part

    @pl.when(step > 0)
    def more():
        grad[...] += part

    @pl.when(step == pl.num_programs(0) - 1)
    def finish():
        put_blocks(grad, tail[...], keep, send)


def grad_kernel(n_region, targets, slots, *refs):
    scores, rest = refs[:n_region], refs[n_region:]
    ids, flows, first, act, w_out, pre_out, tail_out, keep, send, grad, gout, sums = rest
    step = pl.program_id(0)
    cols = act.shape[0]
    rows = keep.shape[1] - TAIL
    lines, lanes = ids.shape[1:]

    @pl.when(step == 0)
    def clear():
        grad[...] = jnp.zeros_like(grad)
        gout[...] = jnp.zeros_like(gout)
        sums[...] = jnp.zeros_like(sums)

    left = lax.broadcasted_iota(jnp.int32, (lines, lanes), 1) < slots

    def halves(reduce, value, rest):
        low = reduce(jnp.where(left, value, rest), axis=1, keepdims=True)
        high = reduce(jnp.where(left, rest, value), axis=1, keepdims=True)
        return jnp.where(left, low, high)

    weight = jnp.broadcast_to(w_out[...], (cols, lanes))
    gained = gout[...]
    trips, numer = sums[0], sums[1]
    for n in range(act.shape[1] // (lines * lanes)):
        score = scores[0][n * lines : (n + 1) * lines, :]
        for k in range(1, n_region):
            at = (n ^ k) * lines if scores[k].shape[0] > lines else 0
            score = score + scores[k][at : at + lines, :]
        valid = ids[step + n] >= 0
        top = halves(jnp.max, jnp.where(valid, score, -jnp.inf), -jnp.inf)
        expo = jnp.where(valid, jnp.exp(score - top), 0.0)
        mass = halves(jnp.sum, expo, 0.0)
        probs = expo / mass
        logp = score - top - jnp.log(mass)
        flow = flows[step + n]
        anchor_total = halves(jnp.sum, flow, 0.0)
        sgrad = jnp.where(valid, probs * anchor_total - flow, 0.0)
        trips = trips + flow
        numer = numer - jnp.where(valid, flow * logp, 0.0)
        for q in range(lines):
            line = sgrad[q : q + 1, :]
            at = slice((n * lines + q) * lanes, (n * lines + q + 1) * lanes)
            active = act[:, at].astype(F32)
            gained = gained + active * line
            pre_out[:, at] = jnp.where(active > 0, weight * line, 0.0).astype(BF)
    gout[...] = gained
    sums[0] = trips
    sums[1] = numer
    grad[...] += lax.dot_general(
        target_rows(first, targets, rows, cols), pre_out[...], (((1,), (1,)), ((), ())), preferred_element_type=F32
    )

    @pl.when(step == pl.num_programs(0) - 1)
    def finish():
        out = jnp.sum(gout[...].T, axis=0, keepdims=True)
        total = jnp.sum(sums[0])
        numer = jnp.sum(sums[1])
        row = lax.broadcasted_iota(jnp.int32, (8, cols), 0)
        lane = lax.broadcasted_iota(jnp.int32, (8, cols), 1)
        stats = jnp.where(lane == 0, total, jnp.where(lane == 1, numer, 0.0))
        tail = pack_tail(jnp.where(row == 0, out, jnp.where(row == 1, stats, 0.0)))
        tail_out[...] = tail
        put_blocks(grad, tail, keep, send)


def core_sum_kernel(keep, received, *outs):
    for j, out in enumerate(outs):
        rows = out.shape[0] - TAIL
        out[:rows, :] = (keep[j, :rows, :].astype(F32) + received[j, :rows, :].astype(F32)).astype(BF)
        out[rows:, :] = pack_tail(unpack_tail(keep[j, rows:, :]) + unpack_tail(received[j, rows:, :]))


def z_sum_kernel(steps, *refs):
    blocks, (out, tails) = refs[:-2], refs[-2:]
    n_z = len(blocks)
    rows = out.shape[0] - TAIL
    total = blocks[0][:rows, :].astype(F32)
    for block in blocks[1:]:
        total = total + block[:rows, :].astype(F32)
    out[:rows, :] = total.astype(BF)
    for j, block in zip(steps, blocks):
        tails[j] = unpack_tail(block[rows:, :])
    z = lax.axis_index("shard") // 2
    tail = tails[z]
    for z_at in range(1, n_z):
        tail = tail + tails[z ^ z_at]
    out[rows:, :] = pack_tail(tail)


def finish_kernel(*refs):
    blocks, (grad, out_grad, loss, held) = refs[:-4], refs[-4:]
    n_region = len(blocks)
    cols = blocks[0].shape[1]
    rows = grad.shape[0]
    for i, block in enumerate(blocks):
        held[i] = block[...]
    region = lax.axis_index("region")
    stats = unpack_tail(held[region][rows:, :])
    total = stats[1:2, 0:1]
    numer = stats[1:2, 1:2]
    loss[...] = numer / total
    inverse = 1.0 / total
    for q in range(n_region):
        block = held[region ^ q]
        grad[:, q * cols : (q + 1) * cols] = block[:rows, :].astype(F32) * inverse
        out_grad[:, q * cols : (q + 1) * cols] = unpack_tail(block[rows:, :])[0:1, :] * inverse


def shards(tiles, tile_block, neighbors, counts, flows, w_anchor, w_dest, w_hidden, w_out):
    blk = counts.shape[0]
    slots = neighbors.shape[1]
    n_region = lax.axis_size("region")
    n_shard = lax.axis_size("shard")
    n_z = n_shard // 2
    hidden = w_hidden.shape[1]
    rows_in = w_anchor.shape[0]
    depth = rows_in * n_shard
    cols = hidden // n_region
    pairs = blk * slots
    lines = pairs // 128
    window = (2 * REACH + 1) * blk
    region = lax.axis_index("region")

    def cut(array, i):
        return lax.dynamic_slice_in_dim(array, (region ^ i) * cols, cols, array.ndim - 1)

    def along_rows(features):
        return [features[:, t * cols : (t + 1) * cols] for t in range(depth // cols)]

    piece = jnp.concatenate([cut(w_anchor, 0), cut(w_dest, 0)], axis=0)

    piece, tile_block = lax.optimization_barrier((piece, tile_block))
    onehot = (tile_block[None, :] == jnp.arange(blk, dtype=jnp.int32)[:, None]).astype(BF)
    sums = jnp.dot(onehot, tiles, preferred_element_type=F32)
    scale = lax.rsqrt(jnp.mean(sums * sums, axis=-1, keepdims=True) + 1e-05)
    features = jnp.concatenate(along_rows((sums * scale).astype(BF)), axis=0)

    payload = jnp.concatenate([piece, features], axis=0)
    from_z = [along_z(payload if j in next_steps(n_z) else piece, j) for j in range(1, n_z)]
    w_anchor, w_dest, payload = lax.optimization_barrier((w_anchor, w_dest, payload))
    raw = jnp.stack([jnp.concatenate([cut(w_anchor, i), cut(w_dest, i)], axis=0) for i in range(n_region)])

    spot = neighbors % (blk * n_shard) - (lax.axis_index("shard") - REACH) * blk
    valid = jnp.arange(slots, dtype=jnp.int32)[None, :] < counts[:, None]
    slot_table = jnp.concatenate([jnp.where(valid, spot, -1), flows], axis=1 if cols >= 2 * slots else 0).astype(BF)
    slot_table = jnp.pad(slot_table, ((0, 0), (0, cols - slot_table.shape[1])))

    held = 2 * rows_in
    around = [features] + [from_z[j - 1][held:] for j in next_steps(n_z)]
    shared = jnp.concatenate([p[rows_in:held] for p in from_z] + around + [slot_table], axis=0)
    plane = jnp.concatenate([shared] + [p[:rows_in] for p in from_z], axis=0)
    planes = [plane] + [swap_region(plane, i) for i in range(1, n_region - 1)] + [swap_region(shared, n_region - 1)]

    mid_raw = cut(w_hidden, 0)
    far_plane = swap_core(plane)
    mid_send, far_plane = lax.optimization_barrier(
        (jnp.concatenate([mid_raw, cut(w_anchor, n_region - 1)], axis=0), far_plane)
    )
    mids = jnp.concatenate([mid_raw] + [along_z(mid_send, j) for j in range(1, n_z)][::-1], axis=0)
    mine = [raw, mids, *planes]
    other = [swap_core(raw), swap_core(mids), far_plane] + [swap_core(x) for x in planes[1:]]
    weight_out = cut(w_out, 0).astype(F32).reshape(cols, 1)

    resident = 2 * hidden * n_region * pairs <= 12 * MIB

    steps = 1 if resident else n_region
    by_lines = VMEM if resident else pl.BlockSpec((lines, 128), lambda i: (i, 0))

    def by_pairs(rows):
        return VMEM if resident else pl.BlockSpec((rows, pairs), lambda i: (0, i))

    first, act, score, ids, flow = pl.pallas_call(
        functools.partial(score_kernel, n_region, n_z, blk, slots),
        grid=(steps,),
        in_specs=[VMEM] * (2 * len(mine) + 1),
        out_specs=[by_pairs(hidden), by_pairs(cols), by_lines, VMEM, VMEM],
        scratch_shapes=[
            pltpu.VMEM((n_region * window, depth), BF),
            pltpu.VMEM((n_region * blk, depth), BF),
            pltpu.VMEM((n_region, depth, 2 * cols), BF),
            pltpu.VMEM((hidden, cols), BF),
            pltpu.VMEM((cols, hidden), BF),
            pltpu.VMEM((n_region, 2 * (window + blk), hidden), BF),
            pltpu.VMEM((n_region, hidden, 2 * (window + blk)), BF),
            pltpu.VMEM((blk, 2 * slots), F32),
        ],
        out_shape=[
            jax.ShapeDtypeStruct((hidden, n_region * pairs), BF),
            jax.ShapeDtypeStruct((cols, n_region * pairs), BF),
            jax.ShapeDtypeStruct((n_region * lines, 128), F32),
            jax.ShapeDtypeStruct((n_region, lines, 128), F32),
            jax.ShapeDtypeStruct((n_region, lines, 128), F32),
        ],
        compiler_params=room(14 + 1.25 * n_region),
        name="scores",
    )(*mine, *other, weight_out)

    parts = [score] + [swap_region(score, i) for i in range(1, n_region)]
    rows = hidden // n_shard
    block = jax.ShapeDtypeStruct((rows + TAIL, cols), BF)
    order = list(range(n_z))[::-1]
    early, later, last = order[: n_z // 2], order[n_z // 2 : -1], order[-1:]

    def blocks(targets):
        return jax.ShapeDtypeStruct((len(targets), rows + TAIL, cols), BF)

    def core_sum(keep, received):
        return pl.pallas_call(
            core_sum_kernel,
            in_specs=[VMEM] * 2,
            out_specs=[VMEM] * keep.shape[0],
            out_shape=[block] * keep.shape[0],
            compiler_params=room(4),
            name="core_sum",
        )(keep, received)

    def rest(targets, pre):
        return pl.pallas_call(
            functools.partial(rest_kernel, targets),
            grid=(steps,),
            in_specs=[by_pairs(hidden), by_pairs(cols), VMEM],
            out_specs=[VMEM] * 2,
            scratch_shapes=[pltpu.VMEM((len(targets) * 2 * rows, cols), F32)],
            out_shape=[blocks(targets)] * 2,
            compiler_params=room(14),
            name="gradient_rest",
        )(first, pre, tail)

    pre, tail, keep, send = pl.pallas_call(
        functools.partial(grad_kernel, n_region, early, slots),
        grid=(steps,),
        in_specs=[
            VMEM if resident else pl.BlockSpec((lines, 128), functools.partial(lambda k, i: (i ^ k, 0), k))
            for k in range(n_region)
        ]
        + [VMEM, VMEM, by_pairs(hidden), by_pairs(cols), VMEM],
        out_specs=[by_pairs(cols)] + [VMEM] * 3,
        scratch_shapes=[
            pltpu.VMEM((len(early) * 2 * rows, cols), F32),
            pltpu.VMEM((cols, 128), F32),
            pltpu.VMEM((2, lines, 128), F32),
        ],
        out_shape=[
            jax.ShapeDtypeStruct((cols, n_region * pairs), BF),
            jax.ShapeDtypeStruct((TAIL, cols), BF),
            blocks(early),
            blocks(early),
        ],
        compiler_params=room(14),
        name="gradient",
    )(*parts, ids, flow, first, act, weight_out)
    received = swap_core(send)
    keep_later, send_later = rest(later, pre)
    sums = core_sum(keep, received)
    pre, *sums = lax.optimization_barrier((pre, *sums))
    received_later = swap_core(send_later)
    keep_last, send_last = rest(last, pre)
    received_last = swap_core(send_last)
    keep_later, received_later, keep_last = lax.optimization_barrier((keep_later, received_later, keep_last))
    sums = lax.optimization_barrier((*sums, *core_sum(keep_later, received_later)))
    arrived = [along_z(x, j) for x, j in zip(sums, early + later)]
    own_rows = [*core_sum(keep_last, received_last)] + arrived
    reduced = pl.pallas_call(
        functools.partial(z_sum_kernel, last + early + later),
        in_specs=[VMEM] * n_z,
        out_specs=VMEM,
        out_shape=block,
        scratch_shapes=[pltpu.VMEM((n_z, 8, cols), F32)],
        compiler_params=room(4),
        name="z_sum",
    )(*own_rows)
    final = [reduced] + [swap_region(reduced, i) for i in range(1, n_region)]
    hidden_grad, out_grad, loss = pl.pallas_call(
        finish_kernel,
        in_specs=[VMEM] * n_region,
        out_specs=[VMEM] * 3,
        out_shape=[
            jax.ShapeDtypeStruct((rows, hidden), F32),
            jax.ShapeDtypeStruct((1, hidden), F32),
            jax.ShapeDtypeStruct((1, 1), F32),
        ],
        scratch_shapes=[pltpu.VMEM((n_region, rows + TAIL, cols), BF)],
        compiler_params=room(4),
        name="finish",
    )(*final)
    return (hidden_grad, out_grad.reshape(hidden), loss.reshape(()))


def solution(mesh):
    return jax.shard_map(
        shards,
        mesh=mesh,
        in_specs=(
            P(("region", "shard"), None),
            P(("region", "shard")),
            P(("region", "shard"), None),
            P(("region", "shard")),
            P(("region", "shard"), None),
            P("shard", None),
            P("shard", None),
            P("shard", None),
            P(),
        ),
        out_specs=(P("shard", None), P(), P()),
        check_vma=False,
    )
```

```python
import functools

import jax
import jax.numpy as jnp
from jax import lax
from jax.experimental import pallas as pl
from jax.experimental.pallas import tpu as pltpu
from jax.sharding import PartitionSpec as P

BF = jnp.bfloat16
F32 = jnp.float32
REACH = 2
TAIL = 16
MIB = 1024 * 1024
VMEM = pl.BlockSpec(memory_space=pltpu.VMEM)


def along_z(array, by):
    devices = lax.axis_size("shard")
    return lax.ppermute(array, "shard", [(i, i ^ (2 * by)) for i in range(devices)])


def next_steps(n_z):
    return [j for j in range(1, n_z) if j & (j + 1) == 0]


def swap_core(array):
    devices = lax.axis_size("shard")
    return lax.ppermute(array, "shard", [(i, i ^ 1) for i in range(devices)])


def swap_region(array, by):
    devices = lax.axis_size("region")
    return lax.ppermute(array, "region", [(i, i ^ by) for i in range(devices)])


def room(mib):
    return pltpu.CompilerParams(vmem_limit_bytes=int(mib * MIB))


def identity(n):
    same = lax.broadcasted_iota(jnp.int32, (n, n), 0) == lax.broadcasted_iota(jnp.int32, (n, n), 1)
    return jnp.where(same, 1.0, 0.0).astype(BF)


def turned(one, array):
    return lax.dot_general(one, array, (((1,), (1,)), ((), ())), preferred_element_type=F32).astype(BF)


def split(value):
    high = value.astype(BF)
    return high, (value - high.astype(F32)).astype(BF)


def pack_tail(sums):
    high, low = split(sums)
    return jnp.concatenate([high.astype(F32), low.astype(F32)], axis=0).astype(BF)


def unpack_tail(rows):
    wide = rows.astype(F32)
    return wide[:8] + wide[8:]


def unit_rows(shard_at, rows, cols, region):
    first = shard_at * rows
    return pl.ds(pl.multiple_of(((first // cols) ^ region) * cols + first % cols, rows), rows)


def score_kernel(n_region, n_z, blk, *refs):
    half = 2 + n_region
    mine, other, rest = refs[:half], refs[half : 2 * half], refs[2 * half :]
    w_out, first_out, act_out, score_out, win_out, feat, own, w_in, w_mid, w_mid_t, anchors, dests = rest
    step = pl.program_id(0)
    region = lax.axis_index("region")
    shard = lax.axis_index("shard")
    z, core = shard // 2, shard % 2
    window = (2 * REACH + 1) * blk
    hidden, cols = w_mid.shape
    parts = feat.shape[1] // cols

    @pl.when(step == 0)
    def assemble():
        raw_cut = mine[0].shape[1] // 2
        dest_rows = (n_z - 1) * raw_cut
        steps = next_steps(n_z)
        feat_rows = (1 + len(steps)) * parts * blk
        slot_row = dest_rows + feat_rows
        slot_rows = -(-window // cols) * blk
        anchor_base = slot_row + slot_rows
        for source, core_at in ((mine, core), (other, 1 - core)):
            raw, mids, planes = source[0], source[1], source[2:]
            rows_mid = hidden // (2 * n_z)
            for j in range(n_z):
                shard_at = 2 * (z ^ j) + core_at
                at = pl.ds(pl.multiple_of(shard_at * raw_cut, raw_cut), raw_cut)
                mid = rows_mid + (n_z - 1 - j) * (rows_mid + raw_cut) if j > 0 else 0
                w_mid[unit_rows(shard_at, rows_mid, cols, z), :] = mids[mid : mid + rows_mid, :]
                for i in range(n_region):
                    base = (j - 1) * raw_cut
                    if j == 0:
                        w_in[i, at, :cols] = raw[i, :raw_cut, :]
                        w_in[i, at, cols:] = raw[i, raw_cut:, :]
                    else:
                        if i == n_region - 1:
                            w_in[i, at, :cols] = mids[mid + rows_mid : mid + rows_mid + raw_cut, :]
                        else:
                            w_in[i, at, :cols] = planes[i][anchor_base + base : anchor_base + base + raw_cut, :]
                        w_in[i, at, cols:] = planes[i][base : base + raw_cut, :]
        one = identity(cols)
        w_mid_t[...] = turned(one, w_mid[...])
        below_at = sum(jnp.where((z ^ (z - 1)) >= j, 1, 0) for j in steps)
        above_at = sum(jnp.where((z ^ (z + 1)) >= j, 1, 0) for j in steps)
        for i in range(n_region):
            near, far = mine[2 + i], other[2 + i]
            for t in range(parts):
                below, here, above = (
                    pl.ds(pl.multiple_of(dest_rows + (k * parts + t) * blk, blk), blk) for k in (below_at, 0, above_at)
                )
                lanes = slice(t * cols, (t + 1) * cols)
                before = jnp.where(core == 0, far[below, :], far[here, :])
                after = jnp.where(core == 0, far[here, :], far[above, :])
                for k, part in enumerate((near[below, :], before, near[here, :], after, near[above, :])):
                    feat[i * window + k * blk : i * window + (k + 1) * blk, lanes] = part
                own[i * blk : (i + 1) * blk, lanes] = near[here, :]
            spans = [
                near[slot_row + at : slot_row + at + blk, : min(cols, window - at // blk * cols)].astype(F32)
                for at in range(0, slot_rows, blk)
            ]
            win_out[i] = jnp.concatenate(spans + [jnp.zeros((blk, 128 - window), F32)], axis=1)
        for i in range(n_region):
            at = region ^ i ^ z
            dests[at] = jnp.dot(feat[...], w_in[i, :, cols:], preferred_element_type=F32)
            anchors[at] = jnp.dot(own[...], w_in[i, :, :cols], preferred_element_type=F32)

    group = 8
    pairs = group * window
    weight = w_out[...]
    for n in range(first_out.shape[0] // (blk * window)):
        reach_at = pl.ds(pl.multiple_of((step + n) * window, window), window)
        own_at = pl.ds(pl.multiple_of((step + n) * blk, blk), blk)
        for c in range(0, blk, group):
            base = (n * blk + c) * window
            for k in range(n_region):
                dest = dests[k, reach_at, :]
                line = anchors[k, own_at, :]
                for a in range(group):
                    total = dest + line[c + a : c + a + 1, :]
                    at = slice(base + a * window, base + (a + 1) * window)
                    first_out[at, k * cols : (k + 1) * cols] = jnp.maximum(total.astype(BF), 0)
            second = lax.dot_general(
                w_mid_t[...], first_out[base : base + pairs, :], (((1,), (1,)), ((), ())), preferred_element_type=F32
            )
            active = jnp.maximum(second, 0.0)
            act_out[:, base : base + pairs] = active.astype(BF)
            score = jnp.sum(active * weight, axis=0, keepdims=True)
            for a in range(group):
                row = n * blk + c + a
                score_out[row : row + 1, :] = jnp.concatenate(
                    [score[:, a * window : (a + 1) * window], jnp.zeros((1, 128 - window), F32)], axis=1
                )


def add_targets(grad, pre, first, targets, width):
    for n, j in enumerate(targets):
        grad[n] += jnp.dot(pre[...], first[:, j * width : (j + 1) * width], preferred_element_type=F32)


def put_blocks(grad, turn, tail, keep, send):
    rows = keep.shape[1] - TAIL
    core = lax.axis_index("shard") % 2
    for n in range(keep.shape[0]):
        turn[n] = grad[n].T
        for target, core_at in ((keep, core), (send, 1 - core)):
            target[n, :rows, :] = turn[n, pl.ds(pl.multiple_of(core_at * rows, rows), rows), :].astype(BF)
            target[n, rows:, :] = tail


def rest_kernel(targets, *refs):
    first, pre, tail, keep, send, grad, turn = refs

    @pl.when(pl.program_id(0) == 0)
    def clear():
        grad[...] = jnp.zeros_like(grad)

    add_targets(grad, pre, first, targets, grad.shape[2])

    @pl.when(pl.program_id(0) == pl.num_programs(0) - 1)
    def finish():
        put_blocks(grad, turn, tail[...], keep, send)


def grad_kernel(n_region, targets, window, *refs):
    scores, rest = refs[:n_region], refs[n_region:]
    win, first, act, w_out, pre_out, tail_out, keep, send, grad, turn, gout, sums = rest
    step = pl.program_id(0)
    cols = act.shape[0]
    blk = win.shape[1]

    @pl.when(step == 0)
    def clear():
        grad[...] = jnp.zeros_like(grad)
        gout[...] = jnp.zeros_like(gout)
        sums[...] = jnp.zeros_like(sums)

    weight = jnp.broadcast_to(w_out[...], (cols, 128))
    gained = gout[...]
    trips, numer = sums[0], sums[1]
    group = 8
    for n in range(act.shape[1] // (blk * window)):
        score = scores[0][n * blk : (n + 1) * blk, :]
        for k in range(1, n_region):
            at = (n ^ k) * blk if scores[k].shape[0] > blk else 0
            score = score + scores[k][at : at + blk, :]
        table = win[step + n]
        valid = table > 0
        flow = jnp.where(valid, table - 1.0, 0.0)
        top = jnp.max(jnp.where(valid, score, -jnp.inf), axis=1, keepdims=True)
        expo = jnp.where(valid, jnp.exp(score - top), 0.0)
        mass = jnp.sum(expo, axis=1, keepdims=True)
        probs = expo / mass
        logp = score - top - jnp.log(mass)
        anchor_total = jnp.sum(flow, axis=1, keepdims=True)
        sgrad = jnp.where(valid, probs * anchor_total - flow, 0.0)
        trips = trips + flow
        numer = numer - jnp.where(valid, flow * logp, 0.0)
        for c in range(0, blk, group):
            wide = jnp.concatenate([sgrad[c + a : c + a + 1, :window] for a in range(group)], axis=1)
            for q in range(0, group * window, 128):
                line = wide[:, q : q + 128]
                at = slice((n * blk + c) * window + q, (n * blk + c) * window + q + 128)
                active = act[:, at].astype(F32)
                gained = gained + active * line
                pre_out[:, at] = jnp.where(active > 0, weight * line, 0.0).astype(BF)
    gout[...] = gained
    sums[0] = trips
    sums[1] = numer
    add_targets(grad, pre_out, first, targets, grad.shape[2])

    @pl.when(step == pl.num_programs(0) - 1)
    def finish():
        out = jnp.sum(gout[...].T, axis=0, keepdims=True)
        total = jnp.sum(sums[0])
        numer = jnp.sum(sums[1])
        row = lax.broadcasted_iota(jnp.int32, (8, cols), 0)
        lane = lax.broadcasted_iota(jnp.int32, (8, cols), 1)
        stats = jnp.where(lane == 0, total, jnp.where(lane == 1, numer, 0.0))
        tail = pack_tail(jnp.where(row == 0, out, jnp.where(row == 1, stats, 0.0)))
        tail_out[...] = tail
        put_blocks(grad, turn, tail, keep, send)


def core_sum_kernel(keep, received, *outs):
    for j, out in enumerate(outs):
        rows = out.shape[0] - TAIL
        out[:rows, :] = (keep[j, :rows, :].astype(F32) + received[j, :rows, :].astype(F32)).astype(BF)
        out[rows:, :] = pack_tail(unpack_tail(keep[j, rows:, :]) + unpack_tail(received[j, rows:, :]))


def z_sum_kernel(steps, *refs):
    blocks, (out, tails) = refs[:-2], refs[-2:]
    n_z = len(blocks)
    rows = out.shape[0] - TAIL
    total = blocks[0][:rows, :].astype(F32)
    for block in blocks[1:]:
        total = total + block[:rows, :].astype(F32)
    out[:rows, :] = total.astype(BF)
    for j, block in zip(steps, blocks):
        tails[j] = unpack_tail(block[rows:, :])
    z = lax.axis_index("shard") // 2
    tail = tails[z]
    for z_at in range(1, n_z):
        tail = tail + tails[z ^ z_at]
    out[rows:, :] = pack_tail(tail)


def finish_kernel(*refs):
    blocks, (grad, out_grad, loss, held) = refs[:-4], refs[-4:]
    n_region = len(blocks)
    cols = blocks[0].shape[1]
    rows = grad.shape[0]
    for i, block in enumerate(blocks):
        held[i] = block[...]
    region = lax.axis_index("region")
    stats = unpack_tail(held[region][rows:, :])
    total = stats[1:2, 0:1]
    numer = stats[1:2, 1:2]
    loss[...] = numer / total
    inverse = 1.0 / total
    for q in range(n_region):
        block = held[region ^ q]
        grad[:, q * cols : (q + 1) * cols] = block[:rows, :].astype(F32) * inverse
        out_grad[:, q * cols : (q + 1) * cols] = unpack_tail(block[rows:, :])[0:1, :] * inverse


def shards(tiles, tile_block, neighbors, counts, flows, w_anchor, w_dest, w_hidden, w_out):
    blk = counts.shape[0]
    slots = neighbors.shape[1]
    n_region = lax.axis_size("region")
    n_shard = lax.axis_size("shard")
    n_z = n_shard // 2
    hidden = w_hidden.shape[1]
    rows_in = w_anchor.shape[0]
    depth = rows_in * n_shard
    cols = hidden // n_region
    window = (2 * REACH + 1) * blk
    pairs = blk * window
    region = lax.axis_index("region")

    def cut(array, i):
        return lax.dynamic_slice_in_dim(array, (region ^ i) * cols, cols, array.ndim - 1)

    def along_rows(features):
        return [features[:, t * cols : (t + 1) * cols] for t in range(depth // cols)]

    piece = jnp.concatenate([cut(w_anchor, 0), cut(w_dest, 0)], axis=0)

    piece, tile_block = lax.optimization_barrier((piece, tile_block))
    onehot = (tile_block[None, :] == jnp.arange(blk, dtype=jnp.int32)[:, None]).astype(BF)
    sums = jnp.dot(onehot, tiles, preferred_element_type=F32)
    scale = lax.rsqrt(jnp.mean(sums * sums, axis=-1, keepdims=True) + 1e-05)
    features = jnp.concatenate(along_rows((sums * scale).astype(BF)), axis=0)

    payload = jnp.concatenate([piece, features], axis=0)
    from_z = [along_z(payload if j in next_steps(n_z) else piece, j) for j in range(1, n_z)]
    w_anchor, w_dest, payload = lax.optimization_barrier((w_anchor, w_dest, payload))
    raw = jnp.stack([jnp.concatenate([cut(w_anchor, i), cut(w_dest, i)], axis=0) for i in range(n_region)])

    spot = neighbors % (blk * n_shard) - (lax.axis_index("shard") - REACH) * blk
    valid = jnp.arange(slots, dtype=jnp.int32)[None, :] < counts[:, None]
    held_by = (spot[:, :, None] == jnp.arange(window, dtype=jnp.int32)) & valid[:, :, None]
    slot_table = jnp.sum(jnp.where(held_by, flows[:, :, None] + 1, 0), axis=1).astype(BF)
    slot_table = jnp.pad(slot_table, ((0, 0), (0, -window % cols)))
    slot_table = jnp.concatenate([slot_table[:, k : k + cols] for k in range(0, slot_table.shape[1], cols)], axis=0)

    held = 2 * rows_in
    around = [features] + [from_z[j - 1][held:] for j in next_steps(n_z)]
    shared = jnp.concatenate([p[rows_in:held] for p in from_z] + around + [slot_table], axis=0)
    plane = jnp.concatenate([shared] + [p[:rows_in] for p in from_z], axis=0)
    planes = [plane] + [swap_region(plane, i) for i in range(1, n_region - 1)] + [swap_region(shared, n_region - 1)]

    mid_raw = cut(w_hidden, 0)
    far_plane = swap_core(plane)
    mid_send, far_plane = lax.optimization_barrier(
        (jnp.concatenate([mid_raw, cut(w_anchor, n_region - 1)], axis=0), far_plane)
    )
    mids = jnp.concatenate([mid_raw] + [along_z(mid_send, j) for j in range(1, n_z)][::-1], axis=0)
    mine = [raw, mids, *planes]
    other = [swap_core(raw), swap_core(mids), far_plane] + [swap_core(x) for x in planes[1:]]
    weight_out = cut(w_out, 0).astype(F32).reshape(cols, 1)

    resident = 2 * hidden * n_region * pairs <= 12 * MIB

    steps = 1 if resident else n_region
    by_anchors = VMEM if resident else pl.BlockSpec((blk, 128), lambda i: (i, 0))

    def by_pairs(rows):
        return VMEM if resident else pl.BlockSpec((rows, pairs), lambda i: (0, i))

    pair_rows = VMEM if resident else pl.BlockSpec((pairs, hidden), lambda i: (i, 0))

    first, act, score, win = pl.pallas_call(
        functools.partial(score_kernel, n_region, n_z, blk),
        grid=(steps,),
        in_specs=[VMEM] * (2 * len(mine) + 1),
        out_specs=[pair_rows, by_pairs(cols), by_anchors, VMEM],
        scratch_shapes=[
            pltpu.VMEM((n_region * window, depth), BF),
            pltpu.VMEM((n_region * blk, depth), BF),
            pltpu.VMEM((n_region, depth, 2 * cols), BF),
            pltpu.VMEM((hidden, cols), BF),
            pltpu.VMEM((cols, hidden), BF),
            pltpu.VMEM((n_region, n_region * blk, cols), F32),
            pltpu.VMEM((n_region, n_region * window, cols), F32),
        ],
        out_shape=[
            jax.ShapeDtypeStruct((n_region * pairs, hidden), BF),
            jax.ShapeDtypeStruct((cols, n_region * pairs), BF),
            jax.ShapeDtypeStruct((n_region * blk, 128), F32),
            jax.ShapeDtypeStruct((n_region, blk, 128), F32),
        ],
        compiler_params=room(14 + 1.25 * n_region),
        name="scores",
    )(*mine, *other, weight_out)

    parts = [score] + [swap_region(score, i) for i in range(1, n_region)]
    rows = hidden // n_shard
    block = jax.ShapeDtypeStruct((rows + TAIL, cols), BF)
    order = list(range(n_z))[::-1]
    early, later, last = order[: n_z // 2], order[n_z // 2 : -1], order[-1:]

    def blocks(targets):
        return jax.ShapeDtypeStruct((len(targets), rows + TAIL, cols), BF)

    def core_sum(keep, received):
        return pl.pallas_call(
            core_sum_kernel,
            in_specs=[VMEM] * 2,
            out_specs=[VMEM] * keep.shape[0],
            out_shape=[block] * keep.shape[0],
            compiler_params=room(4),
            name="core_sum",
        )(keep, received)

    def turns(targets):
        return [pltpu.VMEM((len(targets), *x), F32) for x in ((cols, 2 * rows), (2 * rows, cols))]

    def rest(targets, pre):
        return pl.pallas_call(
            functools.partial(rest_kernel, targets),
            grid=(steps,),
            in_specs=[pair_rows, by_pairs(cols), VMEM],
            out_specs=[VMEM] * 2,
            scratch_shapes=turns(targets),
            out_shape=[blocks(targets)] * 2,
            compiler_params=room(14),
            name="gradient_rest",
        )(first, pre, tail)

    pre, tail, keep, send = pl.pallas_call(
        functools.partial(grad_kernel, n_region, early, window),
        grid=(steps,),
        in_specs=[
            VMEM if resident else pl.BlockSpec((blk, 128), functools.partial(lambda k, i: (i ^ k, 0), k))
            for k in range(n_region)
        ]
        + [VMEM, pair_rows, by_pairs(cols), VMEM],
        out_specs=[by_pairs(cols)] + [VMEM] * 3,
        scratch_shapes=turns(early) + [pltpu.VMEM((cols, 128), F32), pltpu.VMEM((2, blk, 128), F32)],
        out_shape=[
            jax.ShapeDtypeStruct((cols, n_region * pairs), BF),
            jax.ShapeDtypeStruct((TAIL, cols), BF),
            blocks(early),
            blocks(early),
        ],
        compiler_params=room(14),
        name="gradient",
    )(*parts, win, first, act, weight_out)
    received = swap_core(send)
    keep_later, send_later = rest(later, pre)
    sums = core_sum(keep, received)
    pre, *sums = lax.optimization_barrier((pre, *sums))
    received_later = swap_core(send_later)
    keep_last, send_last = rest(last, pre)
    received_last = swap_core(send_last)
    keep_later, received_later, keep_last = lax.optimization_barrier((keep_later, received_later, keep_last))
    sums = lax.optimization_barrier((*sums, *core_sum(keep_later, received_later)))
    arrived = [along_z(x, j) for x, j in zip(sums, early + later)]
    own_rows = [*core_sum(keep_last, received_last)] + arrived
    reduced = pl.pallas_call(
        functools.partial(z_sum_kernel, last + early + later),
        in_specs=[VMEM] * n_z,
        out_specs=VMEM,
        out_shape=block,
        scratch_shapes=[pltpu.VMEM((n_z, 8, cols), F32)],
        compiler_params=room(4),
        name="z_sum",
    )(*own_rows)
    final = [reduced] + [swap_region(reduced, i) for i in range(1, n_region)]
    hidden_grad, out_grad, loss = pl.pallas_call(
        finish_kernel,
        in_specs=[VMEM] * n_region,
        out_specs=[VMEM] * 3,
        out_shape=[
            jax.ShapeDtypeStruct((rows, hidden), F32),
            jax.ShapeDtypeStruct((1, hidden), F32),
            jax.ShapeDtypeStruct((1, 1), F32),
        ],
        scratch_shapes=[pltpu.VMEM((n_region, rows + TAIL, cols), BF)],
        compiler_params=room(4),
        name="finish",
    )(*final)
    return (hidden_grad, out_grad.reshape(hidden), loss.reshape(()))


def solution(mesh):
    return jax.shard_map(
        shards,
        mesh=mesh,
        in_specs=(
            P(("region", "shard"), None),
            P(("region", "shard")),
            P(("region", "shard"), None),
            P(("region", "shard")),
            P(("region", "shard"), None),
            P("shard", None),
            P("shard", None),
            P("shard", None),
            P(),
        ),
        out_specs=(P("shard", None), P(), P()),
        check_vma=False,
    )
```

```python
import functools

import jax
import jax.numpy as jnp
from jax import lax
from jax.experimental import pallas as pl
from jax.experimental.pallas import tpu as pltpu
from jax.sharding import PartitionSpec as P

BF = jnp.bfloat16
F32 = jnp.float32
REACH = 2
TAIL = 16
MIB = 1024 * 1024
VMEM = pl.BlockSpec(memory_space=pltpu.VMEM)


def along_z(array, by):
    devices = lax.axis_size("shard")
    return lax.ppermute(array, "shard", [(i, i ^ (2 * by)) for i in range(devices)])


def next_steps(n_z):
    return [j for j in range(1, n_z) if j & (j + 1) == 0]


def swap_core(array):
    devices = lax.axis_size("shard")
    return lax.ppermute(array, "shard", [(i, i ^ 1) for i in range(devices)])


def swap_region(array, by):
    devices = lax.axis_size("region")
    return lax.ppermute(array, "region", [(i, i ^ by) for i in range(devices)])


def room(mib):
    return pltpu.CompilerParams(vmem_limit_bytes=int(mib * MIB))


def identity(n):
    same = lax.broadcasted_iota(jnp.int32, (n, n), 0) == lax.broadcasted_iota(jnp.int32, (n, n), 1)
    return jnp.where(same, 1.0, 0.0).astype(BF)


def turned(one, array):
    return lax.dot_general(one, array, (((1,), (1,)), ((), ())), preferred_element_type=F32).astype(BF)


def split(value):
    high = value.astype(BF)
    return high, (value - high.astype(F32)).astype(BF)


def pack_tail(sums):
    high, low = split(sums)
    return jnp.concatenate([high.astype(F32), low.astype(F32)], axis=0).astype(BF)


def unpack_tail(rows):
    wide = rows.astype(F32)
    return wide[:8] + wide[8:]


def unit_rows(shard_at, rows, cols, region):
    first = shard_at * rows
    return pl.ds(pl.multiple_of(((first // cols) ^ region) * cols + first % cols, rows), rows)


def score_kernel(n_region, n_z, blk, *refs):
    half = 2 + n_region
    mine, other, rest = refs[:half], refs[half : 2 * half], refs[2 * half :]
    w_out, first_out, act_out, score_out, win_out, feat, own, w_in, w_mid, w_mid_t, anchors, dests = rest
    step = pl.program_id(0)
    region = lax.axis_index("region")
    shard = lax.axis_index("shard")
    z, core = shard // 2, shard % 2
    window = (2 * REACH + 1) * blk
    hidden, cols = w_mid.shape
    parts = feat.shape[1] // cols

    @pl.when(step == 0)
    def assemble():
        raw_cut = mine[0].shape[1] // 2
        dest_rows = (n_z - 1) * raw_cut
        steps = next_steps(n_z)
        feat_rows = (1 + len(steps)) * parts * blk
        slot_row = dest_rows + feat_rows
        slot_rows = -(-window // cols) * blk
        anchor_base = slot_row + slot_rows
        for source, core_at in ((mine, core), (other, 1 - core)):
            raw, mids, planes = source[0], source[1], source[2:]
            rows_mid = hidden // (2 * n_z)
            for j in range(n_z):
                shard_at = 2 * (z ^ j) + core_at
                at = pl.ds(pl.multiple_of(shard_at * raw_cut, raw_cut), raw_cut)
                mid = rows_mid + (n_z - 1 - j) * (rows_mid + raw_cut) if j > 0 else 0
                w_mid[unit_rows(shard_at, rows_mid, cols, z), :] = mids[mid : mid + rows_mid, :]
                for i in range(n_region):
                    base = (j - 1) * raw_cut
                    if j == 0:
                        w_in[i, at, :cols] = raw[i, :raw_cut, :]
                        w_in[i, at, cols:] = raw[i, raw_cut:, :]
                    else:
                        if i == n_region - 1:
                            w_in[i, at, :cols] = mids[mid + rows_mid : mid + rows_mid + raw_cut, :]
                        else:
                            w_in[i, at, :cols] = planes[i][anchor_base + base : anchor_base + base + raw_cut, :]
                        w_in[i, at, cols:] = planes[i][base : base + raw_cut, :]
        one = identity(cols)
        w_mid_t[...] = turned(one, w_mid[...])
        below_at = sum(jnp.where((z ^ (z - 1)) >= j, 1, 0) for j in steps)
        above_at = sum(jnp.where((z ^ (z + 1)) >= j, 1, 0) for j in steps)
        for i in range(n_region):
            near, far = mine[2 + i], other[2 + i]
            for t in range(parts):
                below, here, above = (
                    pl.ds(pl.multiple_of(dest_rows + (k * parts + t) * blk, blk), blk) for k in (below_at, 0, above_at)
                )
                lanes = slice(t * cols, (t + 1) * cols)
                before = jnp.where(core == 0, far[below, :], far[here, :])
                after = jnp.where(core == 0, far[here, :], far[above, :])
                for k, part in enumerate((near[below, :], before, near[here, :], after, near[above, :])):
                    feat[i * window + k * blk : i * window + (k + 1) * blk, lanes] = part
                own[i * blk : (i + 1) * blk, lanes] = near[here, :]
            spans = [
                near[slot_row + at : slot_row + at + blk, : min(cols, window - at // blk * cols)].astype(F32)
                for at in range(0, slot_rows, blk)
            ]
            win_out[i] = jnp.concatenate(spans + [jnp.zeros((blk, 128 - window), F32)], axis=1)
        for i in range(n_region):
            at = region ^ i ^ z
            dests[at] = jnp.dot(feat[...], w_in[i, :, cols:], preferred_element_type=F32)
            anchors[at] = jnp.dot(own[...], w_in[i, :, :cols], preferred_element_type=F32)

    group = 16
    pairs = group * window
    weight = w_out[...]
    for n in range(first_out.shape[0] // (blk * window)):
        reach_at = pl.ds(pl.multiple_of((step + n) * window, window), window)
        own_at = pl.ds(pl.multiple_of((step + n) * blk, blk), blk)
        for c in range(0, blk, group):
            base = (n * blk + c) * window
            for k in range(n_region):
                dest = dests[k, reach_at, :]
                line = anchors[k, own_at, :]
                for a in range(group):
                    total = dest + line[c + a : c + a + 1, :]
                    at = slice(base + a * window, base + (a + 1) * window)
                    first_out[at, k * cols : (k + 1) * cols] = jnp.maximum(total.astype(BF), 0)
            second = lax.dot_general(
                w_mid_t[...], first_out[base : base + pairs, :], (((1,), (1,)), ((), ())), preferred_element_type=F32
            )
            active = jnp.maximum(second, 0.0)
            act_out[:, base : base + pairs] = active.astype(BF)
            score = jnp.sum(active * weight, axis=0, keepdims=True)
            for a in range(group):
                row = n * blk + c + a
                score_out[row : row + 1, :] = jnp.concatenate(
                    [score[:, a * window : (a + 1) * window], jnp.zeros((1, 128 - window), F32)], axis=1
                )


def add_targets(grad, pre, first, targets, width):
    for n, j in enumerate(targets):
        grad[n] += jnp.dot(pre[...], first[:, j * width : (j + 1) * width], preferred_element_type=F32)


def put_blocks(grad, turn, tail, keep, send):
    rows = keep.shape[1] - TAIL
    core = lax.axis_index("shard") % 2
    for n in range(keep.shape[0]):
        turn[n] = grad[n].T
        for target, core_at in ((keep, core), (send, 1 - core)):
            target[n, :rows, :] = turn[n, pl.ds(pl.multiple_of(core_at * rows, rows), rows), :].astype(BF)
            target[n, rows:, :] = tail


def rest_kernel(targets, *refs):
    first, pre, tail, keep, send, grad, turn = refs

    @pl.when(pl.program_id(0) == 0)
    def clear():
        grad[...] = jnp.zeros_like(grad)

    add_targets(grad, pre, first, targets, grad.shape[2])

    @pl.when(pl.program_id(0) == pl.num_programs(0) - 1)
    def finish():
        put_blocks(grad, turn, tail[...], keep, send)


def grad_kernel(n_region, targets, window, *refs):
    scores, rest = refs[:n_region], refs[n_region:]
    win, first, act, w_out, pre_out, tail_out, keep, send, grad, turn, gout, sums = rest
    step = pl.program_id(0)
    cols = act.shape[0]
    blk = win.shape[1]

    @pl.when(step == 0)
    def clear():
        grad[...] = jnp.zeros_like(grad)
        gout[...] = jnp.zeros_like(gout)
        sums[...] = jnp.zeros_like(sums)

    weight = jnp.broadcast_to(w_out[...], (cols, 128))
    gained = gout[...]
    trips, numer = sums[0], sums[1]
    group = 8
    for n in range(act.shape[1] // (blk * window)):
        score = scores[0][n * blk : (n + 1) * blk, :]
        for k in range(1, n_region):
            at = (n ^ k) * blk if scores[k].shape[0] > blk else 0
            score = score + scores[k][at : at + blk, :]
        table = win[step + n]
        valid = table > 0
        flow = jnp.where(valid, table - 1.0, 0.0)
        top = jnp.max(jnp.where(valid, score, -jnp.inf), axis=1, keepdims=True)
        expo = jnp.where(valid, jnp.exp(score - top), 0.0)
        mass = jnp.sum(expo, axis=1, keepdims=True)
        probs = expo / mass
        logp = score - top - jnp.log(mass)
        anchor_total = jnp.sum(flow, axis=1, keepdims=True)
        sgrad = jnp.where(valid, probs * anchor_total - flow, 0.0)
        trips = trips + flow
        numer = numer - jnp.where(valid, flow * logp, 0.0)
        for c in range(0, blk, group):
            wide = jnp.concatenate([sgrad[c + a : c + a + 1, :window] for a in range(group)], axis=1)
            for q in range(0, group * window, 128):
                line = wide[:, q : q + 128]
                at = slice((n * blk + c) * window + q, (n * blk + c) * window + q + 128)
                active = act[:, at].astype(F32)
                gained = gained + active * line
                pre_out[:, at] = jnp.where(active > 0, weight * line, 0.0).astype(BF)
    gout[...] = gained
    sums[0] = trips
    sums[1] = numer
    add_targets(grad, pre_out, first, targets, grad.shape[2])

    @pl.when(step == pl.num_programs(0) - 1)
    def finish():
        out = jnp.sum(gout[...].T, axis=0, keepdims=True)
        total = jnp.sum(sums[0])
        numer = jnp.sum(sums[1])
        row = lax.broadcasted_iota(jnp.int32, (8, cols), 0)
        lane = lax.broadcasted_iota(jnp.int32, (8, cols), 1)
        stats = jnp.where(lane == 0, total, jnp.where(lane == 1, numer, 0.0))
        tail = pack_tail(jnp.where(row == 0, out, jnp.where(row == 1, stats, 0.0)))
        tail_out[...] = tail
        put_blocks(grad, turn, tail, keep, send)


def core_sum_kernel(keep, received, *outs):
    for j, out in enumerate(outs):
        rows = out.shape[0] - TAIL
        out[:rows, :] = (keep[j, :rows, :].astype(F32) + received[j, :rows, :].astype(F32)).astype(BF)
        out[rows:, :] = pack_tail(unpack_tail(keep[j, rows:, :]) + unpack_tail(received[j, rows:, :]))


def z_sum_kernel(steps, *refs):
    blocks, (out, tails) = refs[:-2], refs[-2:]
    n_z = len(blocks)
    rows = out.shape[0] - TAIL
    total = blocks[0][:rows, :].astype(F32)
    for block in blocks[1:]:
        total = total + block[:rows, :].astype(F32)
    out[:rows, :] = total.astype(BF)
    for j, block in zip(steps, blocks):
        tails[j] = unpack_tail(block[rows:, :])
    z = lax.axis_index("shard") // 2
    tail = tails[z]
    for z_at in range(1, n_z):
        tail = tail + tails[z ^ z_at]
    out[rows:, :] = pack_tail(tail)


def finish_kernel(*refs):
    blocks, (grad, out_grad, loss, held) = refs[:-4], refs[-4:]
    n_region = len(blocks)
    cols = blocks[0].shape[1]
    rows = grad.shape[0]
    for i, block in enumerate(blocks):
        held[i] = block[...]
    region = lax.axis_index("region")
    stats = unpack_tail(held[region][rows:, :])
    total = stats[1:2, 0:1]
    numer = stats[1:2, 1:2]
    loss[...] = numer / total
    inverse = 1.0 / total
    for q in range(n_region):
        block = held[region ^ q]
        grad[:, q * cols : (q + 1) * cols] = block[:rows, :].astype(F32) * inverse
        out_grad[:, q * cols : (q + 1) * cols] = unpack_tail(block[rows:, :])[0:1, :] * inverse


def shards(tiles, tile_block, neighbors, counts, flows, w_anchor, w_dest, w_hidden, w_out):
    blk = counts.shape[0]
    slots = neighbors.shape[1]
    n_region = lax.axis_size("region")
    n_shard = lax.axis_size("shard")
    n_z = n_shard // 2
    hidden = w_hidden.shape[1]
    rows_in = w_anchor.shape[0]
    depth = rows_in * n_shard
    cols = hidden // n_region
    window = (2 * REACH + 1) * blk
    pairs = blk * window
    region = lax.axis_index("region")

    def cut(array, i):
        return lax.dynamic_slice_in_dim(array, (region ^ i) * cols, cols, array.ndim - 1)

    def along_rows(features):
        return [features[:, t * cols : (t + 1) * cols] for t in range(depth // cols)]

    piece = jnp.concatenate([cut(w_anchor, 0), cut(w_dest, 0)], axis=0)

    piece, tile_block = lax.optimization_barrier((piece, tile_block))
    onehot = (tile_block[None, :] == jnp.arange(blk, dtype=jnp.int32)[:, None]).astype(BF)
    sums = jnp.dot(onehot, tiles, preferred_element_type=F32)
    scale = lax.rsqrt(jnp.mean(sums * sums, axis=-1, keepdims=True) + 1e-05)
    features = jnp.concatenate(along_rows((sums * scale).astype(BF)), axis=0)

    payload = jnp.concatenate([piece, features], axis=0)
    from_z = [along_z(payload if j in next_steps(n_z) else piece, j) for j in range(1, n_z)]
    w_anchor, w_dest, payload = lax.optimization_barrier((w_anchor, w_dest, payload))
    raw = jnp.stack([jnp.concatenate([cut(w_anchor, i), cut(w_dest, i)], axis=0) for i in range(n_region)])

    spot = neighbors % (blk * n_shard) - (lax.axis_index("shard") - REACH) * blk
    valid = jnp.arange(slots, dtype=jnp.int32)[None, :] < counts[:, None]
    held_by = (spot[:, :, None] == jnp.arange(window, dtype=jnp.int32)) & valid[:, :, None]
    slot_table = jnp.sum(jnp.where(held_by, flows[:, :, None] + 1, 0), axis=1).astype(BF)
    slot_table = jnp.pad(slot_table, ((0, 0), (0, -window % cols)))
    slot_table = jnp.concatenate([slot_table[:, k : k + cols] for k in range(0, slot_table.shape[1], cols)], axis=0)

    held = 2 * rows_in
    around = [features] + [from_z[j - 1][held:] for j in next_steps(n_z)]
    shared = jnp.concatenate([p[rows_in:held] for p in from_z] + around + [slot_table], axis=0)
    plane = jnp.concatenate([shared] + [p[:rows_in] for p in from_z], axis=0)
    planes = [plane] + [swap_region(plane, i) for i in range(1, n_region - 1)] + [swap_region(shared, n_region - 1)]

    mid_raw = cut(w_hidden, 0)
    far_plane = swap_core(plane)
    mid_send, far_plane = lax.optimization_barrier(
        (jnp.concatenate([mid_raw, cut(w_anchor, n_region - 1)], axis=0), far_plane)
    )
    mids = jnp.concatenate([mid_raw] + [along_z(mid_send, j) for j in range(1, n_z)][::-1], axis=0)
    mine = [raw, mids, *planes]
    other = [swap_core(raw), swap_core(mids), far_plane] + [swap_core(x) for x in planes[1:]]
    weight_out = cut(w_out, 0).astype(F32).reshape(cols, 1)

    resident = 2 * hidden * n_region * pairs <= 12 * MIB

    steps = 1 if resident else n_region
    by_anchors = VMEM if resident else pl.BlockSpec((blk, 128), lambda i: (i, 0))

    def by_pairs(rows):
        return VMEM if resident else pl.BlockSpec((rows, pairs), lambda i: (0, i))

    pair_rows = VMEM if resident else pl.BlockSpec((pairs, hidden), lambda i: (i, 0))

    first, act, score, win = pl.pallas_call(
        functools.partial(score_kernel, n_region, n_z, blk),
        grid=(steps,),
        in_specs=[VMEM] * (2 * len(mine) + 1),
        out_specs=[pair_rows, by_pairs(cols), by_anchors, VMEM],
        scratch_shapes=[
            pltpu.VMEM((n_region * window, depth), BF),
            pltpu.VMEM((n_region * blk, depth), BF),
            pltpu.VMEM((n_region, depth, 2 * cols), BF),
            pltpu.VMEM((hidden, cols), BF),
            pltpu.VMEM((cols, hidden), BF),
            pltpu.VMEM((n_region, n_region * blk, cols), F32),
            pltpu.VMEM((n_region, n_region * window, cols), F32),
        ],
        out_shape=[
            jax.ShapeDtypeStruct((n_region * pairs, hidden), BF),
            jax.ShapeDtypeStruct((cols, n_region * pairs), BF),
            jax.ShapeDtypeStruct((n_region * blk, 128), F32),
            jax.ShapeDtypeStruct((n_region, blk, 128), F32),
        ],
        compiler_params=room(14 + 1.25 * n_region),
        name="scores",
    )(*mine, *other, weight_out)

    parts = [score] + [swap_region(score, i) for i in range(1, n_region)]
    rows = hidden // n_shard
    block = jax.ShapeDtypeStruct((rows + TAIL, cols), BF)
    order = list(range(n_z))[::-1]
    early, late = order[: n_z // 2], order[n_z // 2 :]

    def blocks(targets):
        return jax.ShapeDtypeStruct((len(targets), rows + TAIL, cols), BF)

    def core_sum(keep, received):
        return pl.pallas_call(
            core_sum_kernel,
            in_specs=[VMEM] * 2,
            out_specs=[VMEM] * keep.shape[0],
            out_shape=[block] * keep.shape[0],
            compiler_params=room(4),
            name="core_sum",
        )(keep, received)

    def turns(targets):
        return [pltpu.VMEM((len(targets), *x), F32) for x in ((cols, 2 * rows), (2 * rows, cols))]

    def rest(targets, pre):
        return pl.pallas_call(
            functools.partial(rest_kernel, targets),
            grid=(steps,),
            in_specs=[pair_rows, by_pairs(cols), VMEM],
            out_specs=[VMEM] * 2,
            scratch_shapes=turns(targets),
            out_shape=[blocks(targets)] * 2,
            compiler_params=room(14),
            name="gradient_rest",
        )(first, pre, tail)

    pre, tail, keep, send = pl.pallas_call(
        functools.partial(grad_kernel, n_region, early, window),
        grid=(steps,),
        in_specs=[
            VMEM if resident else pl.BlockSpec((blk, 128), functools.partial(lambda k, i: (i ^ k, 0), k))
            for k in range(n_region)
        ]
        + [VMEM, pair_rows, by_pairs(cols), VMEM],
        out_specs=[by_pairs(cols)] + [VMEM] * 3,
        scratch_shapes=turns(early) + [pltpu.VMEM((cols, 128), F32), pltpu.VMEM((2, blk, 128), F32)],
        out_shape=[
            jax.ShapeDtypeStruct((cols, n_region * pairs), BF),
            jax.ShapeDtypeStruct((TAIL, cols), BF),
            blocks(early),
            blocks(early),
        ],
        compiler_params=room(14),
        name="gradient",
    )(*parts, win, first, act, weight_out)
    received = swap_core(send)
    keep_late, send_late = rest(late, pre)
    received, keep_late, send_late = lax.optimization_barrier((received, keep_late, send_late))
    sums = core_sum(keep, received)
    arrived = [along_z(x, j) for x, j in zip(sums, early)]
    *nearer, own = core_sum(keep_late, swap_core(send_late))
    arrived += [along_z(x, j) for x, j in zip(nearer, late)]
    own_rows = [own] + arrived
    reduced = pl.pallas_call(
        functools.partial(z_sum_kernel, order[-1:] + order[:-1]),
        in_specs=[VMEM] * n_z,
        out_specs=VMEM,
        out_shape=block,
        scratch_shapes=[pltpu.VMEM((n_z, 8, cols), F32)],
        compiler_params=room(4),
        name="z_sum",
    )(*own_rows)
    final = [reduced] + [swap_region(reduced, i) for i in range(1, n_region)]
    hidden_grad, out_grad, loss = pl.pallas_call(
        finish_kernel,
        in_specs=[VMEM] * n_region,
        out_specs=[VMEM] * 3,
        out_shape=[
            jax.ShapeDtypeStruct((rows, hidden), F32),
            jax.ShapeDtypeStruct((1, hidden), F32),
            jax.ShapeDtypeStruct((1, 1), F32),
        ],
        scratch_shapes=[pltpu.VMEM((n_region, rows + TAIL, cols), BF)],
        compiler_params=room(4),
        name="finish",
    )(*final)
    return (hidden_grad, out_grad.reshape(hidden), loss.reshape(()))


def solution(mesh):
    return jax.shard_map(
        shards,
        mesh=mesh,
        in_specs=(
            P(("region", "shard"), None),
            P(("region", "shard")),
            P(("region", "shard"), None),
            P(("region", "shard")),
            P(("region", "shard"), None),
            P("shard", None),
            P("shard", None),
            P("shard", None),
            P(),
        ),
        out_specs=(P("shard", None), P(), P()),
        check_vma=False,
    )
```

```python
import functools

import jax
import jax.numpy as jnp
from jax import lax
from jax.experimental import pallas as pl
from jax.experimental.pallas import tpu as pltpu
from jax.sharding import PartitionSpec as P

BF = jnp.bfloat16
F32 = jnp.float32
REACH = 2
TAIL = 16
MIB = 1024 * 1024
VMEM = pl.BlockSpec(memory_space=pltpu.VMEM)


def along_z(array, by):
    devices = lax.axis_size("shard")
    return lax.ppermute(array, "shard", [(i, i ^ (2 * by)) for i in range(devices)])


def next_steps(n_z):
    return [j for j in range(1, n_z) if j & (j + 1) == 0]


def swap_core(array):
    devices = lax.axis_size("shard")
    return lax.ppermute(array, "shard", [(i, i ^ 1) for i in range(devices)])


def swap_region(array, by):
    devices = lax.axis_size("region")
    return lax.ppermute(array, "region", [(i, i ^ by) for i in range(devices)])


def room(mib):
    return pltpu.CompilerParams(vmem_limit_bytes=int(mib * MIB))


def identity(n):
    same = lax.broadcasted_iota(jnp.int32, (n, n), 0) == lax.broadcasted_iota(jnp.int32, (n, n), 1)
    return jnp.where(same, 1.0, 0.0).astype(BF)


def turned(one, array):
    return lax.dot_general(one, array, (((1,), (1,)), ((), ())), preferred_element_type=F32).astype(BF)


def split(value):
    high = value.astype(BF)
    return high, (value - high.astype(F32)).astype(BF)


def pack_tail(sums):
    high, low = split(sums)
    return jnp.concatenate([high.astype(F32), low.astype(F32)], axis=0).astype(BF)


def unpack_tail(rows):
    wide = rows.astype(F32)
    return wide[:8] + wide[8:]


def unit_rows(shard_at, rows, cols, region):
    first = shard_at * rows
    return pl.ds(pl.multiple_of(((first // cols) ^ region) * cols + first % cols, rows), rows)


def score_kernel(n_region, n_z, blk, *refs):
    half = 2 + n_region
    mine, other, rest = refs[:half], refs[half : 2 * half], refs[2 * half :]
    w_out, first_out, act_out, score_out, win_out, feat, own, w_in, w_mid, w_mid_t, anchors, dests = rest
    step = pl.program_id(0)
    region = lax.axis_index("region")
    shard = lax.axis_index("shard")
    z, core = shard // 2, shard % 2
    window = (2 * REACH + 1) * blk
    hidden, cols = w_mid.shape
    parts = feat.shape[1] // cols

    @pl.when(step == 0)
    def assemble():
        raw_cut = mine[0].shape[1] // 2
        dest_rows = (n_z - 1) * raw_cut
        steps = next_steps(n_z)
        feat_rows = (1 + len(steps)) * parts * blk
        slot_row = dest_rows + feat_rows
        slot_rows = -(-window // cols) * blk
        anchor_base = slot_row + slot_rows
        for source, core_at in ((mine, core), (other, 1 - core)):
            raw, mids, planes = source[0], source[1], source[2:]
            rows_mid = hidden // (2 * n_z)
            for j in range(n_z):
                shard_at = 2 * (z ^ j) + core_at
                at = pl.ds(pl.multiple_of(shard_at * raw_cut, raw_cut), raw_cut)
                mid = rows_mid + (n_z - 1 - j) * (rows_mid + raw_cut) if j > 0 else 0
                w_mid[unit_rows(shard_at, rows_mid, cols, z), :] = mids[mid : mid + rows_mid, :]
                for i in range(n_region):
                    base = (j - 1) * raw_cut
                    if j == 0:
                        w_in[i, at, :cols] = raw[i, :raw_cut, :]
                        w_in[i, at, cols:] = raw[i, raw_cut:, :]
                    else:
                        if i == n_region - 1:
                            w_in[i, at, :cols] = mids[mid + rows_mid : mid + rows_mid + raw_cut, :]
                        else:
                            w_in[i, at, :cols] = planes[i][anchor_base + base : anchor_base + base + raw_cut, :]
                        w_in[i, at, cols:] = planes[i][base : base + raw_cut, :]
        one = identity(cols)
        w_mid_t[...] = turned(one, w_mid[...])
        below_at = sum(jnp.where((z ^ (z - 1)) >= j, 1, 0) for j in steps)
        above_at = sum(jnp.where((z ^ (z + 1)) >= j, 1, 0) for j in steps)
        for i in range(n_region):
            near, far = mine[2 + i], other[2 + i]
            for t in range(parts):
                below, here, above = (
                    pl.ds(pl.multiple_of(dest_rows + (k * parts + t) * blk, blk), blk) for k in (below_at, 0, above_at)
                )
                lanes = slice(t * cols, (t + 1) * cols)
                before = jnp.where(core == 0, far[below, :], far[here, :])
                after = jnp.where(core == 0, far[here, :], far[above, :])
                for k, part in enumerate((near[below, :], before, near[here, :], after, near[above, :])):
                    feat[i * window + k * blk : i * window + (k + 1) * blk, lanes] = part
                own[i * blk : (i + 1) * blk, lanes] = near[here, :]
            spans = [
                near[slot_row + at : slot_row + at + blk, : min(cols, window - at // blk * cols)].astype(F32)
                for at in range(0, slot_rows, blk)
            ]
            win_out[i] = jnp.concatenate(spans + [jnp.zeros((blk, 128 - window), F32)], axis=1)
        for i in range(n_region):
            at = region ^ i ^ z
            dests[at] = jnp.dot(feat[...], w_in[i, :, cols:], preferred_element_type=F32)
            anchors[at] = jnp.dot(own[...], w_in[i, :, :cols], preferred_element_type=F32)

    weight = w_out[...]
    regions = first_out.shape[0] // (blk * window)
    together = 2 if regions % 2 == 0 else 1
    pairs = together * blk * window
    for n in range(0, regions, together):
        for m in range(n, n + together):
            reach_at = pl.ds(pl.multiple_of((step + m) * window, window), window)
            own_at = pl.ds(pl.multiple_of((step + m) * blk, blk), blk)
            for k in range(n_region):
                dest = dests[k, reach_at, :]
                line = anchors[k, own_at, :]
                for a in range(blk):
                    total = dest + line[a : a + 1, :]
                    at = slice((m * blk + a) * window, (m * blk + a + 1) * window)
                    first_out[at, k * cols : (k + 1) * cols] = jnp.maximum(total.astype(BF), 0)
        base = n * blk * window
        second = lax.dot_general(
            w_mid_t[...], first_out[base : base + pairs, :], (((1,), (1,)), ((), ())), preferred_element_type=F32
        )
        active = jnp.maximum(second, 0.0)
        act_out[:, base : base + pairs] = active.astype(BF)
        score = jnp.sum(active * weight, axis=0, keepdims=True)
        for a in range(together * blk):
            score_out[n * blk + a : n * blk + a + 1, :] = jnp.concatenate(
                [score[:, a * window : (a + 1) * window], jnp.zeros((1, 128 - window), F32)], axis=1
            )


def add_targets(grad, pre, first, targets, width):
    for n, j in enumerate(targets):
        grad[n] += jnp.dot(pre[...], first[:, j * width : (j + 1) * width], preferred_element_type=F32)


def put_blocks(grad, turn, tail, keep, send):
    rows = keep.shape[1] - TAIL
    core = lax.axis_index("shard") % 2
    for n in range(keep.shape[0]):
        turn[n] = grad[n].T
        for target, core_at in ((keep, core), (send, 1 - core)):
            target[n, :rows, :] = turn[n, pl.ds(pl.multiple_of(core_at * rows, rows), rows), :].astype(BF)
            target[n, rows:, :] = tail


def rest_kernel(targets, *refs):
    first, pre, tail, keep, send, grad, turn = refs

    @pl.when(pl.program_id(0) == 0)
    def clear():
        grad[...] = jnp.zeros_like(grad)

    add_targets(grad, pre, first, targets, grad.shape[2])

    @pl.when(pl.program_id(0) == pl.num_programs(0) - 1)
    def finish():
        put_blocks(grad, turn, tail[...], keep, send)


def grad_kernel(n_region, targets, window, *refs):
    scores, rest = refs[:n_region], refs[n_region:]
    win, first, act, w_out, pre_out, tail_out, keep, send, grad, turn, gout, sums = rest
    step = pl.program_id(0)
    cols = act.shape[0]
    blk = win.shape[1]

    @pl.when(step == 0)
    def clear():
        grad[...] = jnp.zeros_like(grad)
        gout[...] = jnp.zeros_like(gout)
        sums[...] = jnp.zeros_like(sums)

    weight = jnp.broadcast_to(w_out[...], (cols, 128))
    gained = gout[...]
    trips, numer = sums[0], sums[1]
    group = 8
    for n in range(act.shape[1] // (blk * window)):
        score = scores[0][n * blk : (n + 1) * blk, :]
        for k in range(1, n_region):
            at = (n ^ k) * blk if scores[k].shape[0] > blk else 0
            score = score + scores[k][at : at + blk, :]
        table = win[step + n]
        valid = table > 0
        flow = jnp.where(valid, table - 1.0, 0.0)
        top = jnp.max(jnp.where(valid, score, -jnp.inf), axis=1, keepdims=True)
        expo = jnp.where(valid, jnp.exp(score - top), 0.0)
        mass = jnp.sum(expo, axis=1, keepdims=True)
        probs = expo / mass
        logp = score - top - jnp.log(mass)
        anchor_total = jnp.sum(flow, axis=1, keepdims=True)
        sgrad = jnp.where(valid, probs * anchor_total - flow, 0.0)
        trips = trips + flow
        numer = numer - jnp.where(valid, flow * logp, 0.0)
        for c in range(0, blk, group):
            wide = jnp.concatenate([sgrad[c + a : c + a + 1, :window] for a in range(group)], axis=1)
            for q in range(0, group * window, 128):
                line = wide[:, q : q + 128]
                at = slice((n * blk + c) * window + q, (n * blk + c) * window + q + 128)
                active = act[:, at].astype(F32)
                gained = gained + active * line
                pre_out[:, at] = jnp.where(active > 0, weight * line, 0.0).astype(BF)
    gout[...] = gained
    sums[0] = trips
    sums[1] = numer
    add_targets(grad, pre_out, first, targets, grad.shape[2])

    @pl.when(step == pl.num_programs(0) - 1)
    def finish():
        out = jnp.sum(gout[...].T, axis=0, keepdims=True)
        total = jnp.sum(sums[0])
        numer = jnp.sum(sums[1])
        row = lax.broadcasted_iota(jnp.int32, (8, cols), 0)
        lane = lax.broadcasted_iota(jnp.int32, (8, cols), 1)
        stats = jnp.where(lane == 0, total, jnp.where(lane == 1, numer, 0.0))
        tail = pack_tail(jnp.where(row == 0, out, jnp.where(row == 1, stats, 0.0)))
        tail_out[...] = tail
        put_blocks(grad, turn, tail, keep, send)


def core_sum_kernel(keep, received, *outs):
    for j, out in enumerate(outs):
        rows = out.shape[0] - TAIL
        out[:rows, :] = (keep[j, :rows, :].astype(F32) + received[j, :rows, :].astype(F32)).astype(BF)
        out[rows:, :] = pack_tail(unpack_tail(keep[j, rows:, :]) + unpack_tail(received[j, rows:, :]))


def z_sum_kernel(steps, *refs):
    blocks, (out, tails) = refs[:-2], refs[-2:]
    n_z = len(blocks)
    rows = out.shape[0] - TAIL
    total = blocks[0][:rows, :].astype(F32)
    for block in blocks[1:]:
        total = total + block[:rows, :].astype(F32)
    out[:rows, :] = total.astype(BF)
    for j, block in zip(steps, blocks):
        tails[j] = unpack_tail(block[rows:, :])
    z = lax.axis_index("shard") // 2
    tail = tails[z]
    for z_at in range(1, n_z):
        tail = tail + tails[z ^ z_at]
    out[rows:, :] = pack_tail(tail)


def finish_kernel(*refs):
    blocks, (grad, out_grad, loss, held) = refs[:-4], refs[-4:]
    n_region = len(blocks)
    cols = blocks[0].shape[1]
    rows = grad.shape[0]
    for i, block in enumerate(blocks):
        held[i] = block[...]
    region = lax.axis_index("region")
    stats = unpack_tail(held[region][rows:, :])
    total = stats[1:2, 0:1]
    numer = stats[1:2, 1:2]
    loss[...] = numer / total
    inverse = 1.0 / total
    for q in range(n_region):
        block = held[region ^ q]
        grad[:, q * cols : (q + 1) * cols] = block[:rows, :].astype(F32) * inverse
        out_grad[:, q * cols : (q + 1) * cols] = unpack_tail(block[rows:, :])[0:1, :] * inverse


def shards(tiles, tile_block, neighbors, counts, flows, w_anchor, w_dest, w_hidden, w_out):
    blk = counts.shape[0]
    slots = neighbors.shape[1]
    n_region = lax.axis_size("region")
    n_shard = lax.axis_size("shard")
    n_z = n_shard // 2
    hidden = w_hidden.shape[1]
    rows_in = w_anchor.shape[0]
    depth = rows_in * n_shard
    cols = hidden // n_region
    window = (2 * REACH + 1) * blk
    pairs = blk * window
    region = lax.axis_index("region")

    def cut(array, i):
        return lax.dynamic_slice_in_dim(array, (region ^ i) * cols, cols, array.ndim - 1)

    def along_rows(features):
        return [features[:, t * cols : (t + 1) * cols] for t in range(depth // cols)]

    piece = jnp.concatenate([cut(w_anchor, 0), cut(w_dest, 0)], axis=0)

    piece, tile_block = lax.optimization_barrier((piece, tile_block))
    onehot = (tile_block[None, :] == jnp.arange(blk, dtype=jnp.int32)[:, None]).astype(BF)
    sums = jnp.dot(onehot, tiles, preferred_element_type=F32)
    scale = lax.rsqrt(jnp.mean(sums * sums, axis=-1, keepdims=True) + 1e-05)
    features = jnp.concatenate(along_rows((sums * scale).astype(BF)), axis=0)

    payload = jnp.concatenate([piece, features], axis=0)
    from_z = [along_z(payload if j in next_steps(n_z) else piece, j) for j in range(1, n_z)]
    w_anchor, w_dest, payload = lax.optimization_barrier((w_anchor, w_dest, payload))
    raw = jnp.stack([jnp.concatenate([cut(w_anchor, i), cut(w_dest, i)], axis=0) for i in range(n_region)])

    spot = neighbors % (blk * n_shard) - (lax.axis_index("shard") - REACH) * blk
    valid = jnp.arange(slots, dtype=jnp.int32)[None, :] < counts[:, None]
    held_by = (spot[:, :, None] == jnp.arange(window, dtype=jnp.int32)) & valid[:, :, None]
    slot_table = jnp.sum(jnp.where(held_by, flows[:, :, None] + 1, 0), axis=1).astype(BF)
    slot_table = jnp.pad(slot_table, ((0, 0), (0, -window % cols)))
    slot_table = jnp.concatenate([slot_table[:, k : k + cols] for k in range(0, slot_table.shape[1], cols)], axis=0)

    held = 2 * rows_in
    around = [features] + [from_z[j - 1][held:] for j in next_steps(n_z)]
    shared = jnp.concatenate([p[rows_in:held] for p in from_z] + around + [slot_table], axis=0)
    plane = jnp.concatenate([shared] + [p[:rows_in] for p in from_z], axis=0)
    planes = [plane] + [swap_region(plane, i) for i in range(1, n_region - 1)] + [swap_region(shared, n_region - 1)]

    mid_raw = cut(w_hidden, 0)
    far_plane = swap_core(plane)
    mid_send, far_plane = lax.optimization_barrier(
        (jnp.concatenate([mid_raw, cut(w_anchor, n_region - 1)], axis=0), far_plane)
    )
    mids = jnp.concatenate([mid_raw] + [along_z(mid_send, j) for j in range(1, n_z)][::-1], axis=0)
    mine = [raw, mids, *planes]
    other = [swap_core(raw), swap_core(mids), far_plane] + [swap_core(x) for x in planes[1:]]
    weight_out = cut(w_out, 0).astype(F32).reshape(cols, 1)

    resident = 2 * hidden * n_region * pairs <= 12 * MIB

    steps = 1 if resident else n_region
    by_anchors = VMEM if resident else pl.BlockSpec((blk, 128), lambda i: (i, 0))

    def by_pairs(rows):
        return VMEM if resident else pl.BlockSpec((rows, pairs), lambda i: (0, i))

    pair_rows = VMEM if resident else pl.BlockSpec((pairs, hidden), lambda i: (i, 0))

    first, act, score, win = pl.pallas_call(
        functools.partial(score_kernel, n_region, n_z, blk),
        grid=(steps,),
        in_specs=[VMEM] * (2 * len(mine) + 1),
        out_specs=[pair_rows, by_pairs(cols), by_anchors, VMEM],
        scratch_shapes=[
            pltpu.VMEM((n_region * window, depth), BF),
            pltpu.VMEM((n_region * blk, depth), BF),
            pltpu.VMEM((n_region, depth, 2 * cols), BF),
            pltpu.VMEM((hidden, cols), BF),
            pltpu.VMEM((cols, hidden), BF),
            pltpu.VMEM((n_region, n_region * blk, cols), F32),
            pltpu.VMEM((n_region, n_region * window, cols), F32),
        ],
        out_shape=[
            jax.ShapeDtypeStruct((n_region * pairs, hidden), BF),
            jax.ShapeDtypeStruct((cols, n_region * pairs), BF),
            jax.ShapeDtypeStruct((n_region * blk, 128), F32),
            jax.ShapeDtypeStruct((n_region, blk, 128), F32),
        ],
        compiler_params=room(14 + 1.25 * n_region),
        name="scores",
    )(*mine, *other, weight_out)

    parts = [score] + [swap_region(score, i) for i in range(1, n_region)]
    rows = hidden // n_shard
    block = jax.ShapeDtypeStruct((rows + TAIL, cols), BF)
    order = list(range(n_z))[::-1]
    early, late = order[: n_z // 2], order[n_z // 2 :]

    def blocks(targets):
        return jax.ShapeDtypeStruct((len(targets), rows + TAIL, cols), BF)

    def core_sum(keep, received):
        return pl.pallas_call(
            core_sum_kernel,
            in_specs=[VMEM] * 2,
            out_specs=[VMEM] * keep.shape[0],
            out_shape=[block] * keep.shape[0],
            compiler_params=room(4),
            name="core_sum",
        )(keep, received)

    def turns(targets):
        return [pltpu.VMEM((len(targets), *x), F32) for x in ((cols, 2 * rows), (2 * rows, cols))]

    def rest(targets, pre):
        return pl.pallas_call(
            functools.partial(rest_kernel, targets),
            grid=(steps,),
            in_specs=[pair_rows, by_pairs(cols), VMEM],
            out_specs=[VMEM] * 2,
            scratch_shapes=turns(targets),
            out_shape=[blocks(targets)] * 2,
            compiler_params=room(14),
            name="gradient_rest",
        )(first, pre, tail)

    pre, tail, keep, send = pl.pallas_call(
        functools.partial(grad_kernel, n_region, early, window),
        grid=(steps,),
        in_specs=[
            VMEM if resident else pl.BlockSpec((blk, 128), functools.partial(lambda k, i: (i ^ k, 0), k))
            for k in range(n_region)
        ]
        + [VMEM, pair_rows, by_pairs(cols), VMEM],
        out_specs=[by_pairs(cols)] + [VMEM] * 3,
        scratch_shapes=turns(early) + [pltpu.VMEM((cols, 128), F32), pltpu.VMEM((2, blk, 128), F32)],
        out_shape=[
            jax.ShapeDtypeStruct((cols, n_region * pairs), BF),
            jax.ShapeDtypeStruct((TAIL, cols), BF),
            blocks(early),
            blocks(early),
        ],
        compiler_params=room(14),
        name="gradient",
    )(*parts, win, first, act, weight_out)
    received = swap_core(send)
    keep_late, send_late = rest(late, pre)
    received, keep_late, send_late = lax.optimization_barrier((received, keep_late, send_late))
    sums = core_sum(keep, received)
    arrived = [along_z(x, j) for x, j in zip(sums, early)]
    *nearer, own = core_sum(keep_late, swap_core(send_late))
    arrived += [along_z(x, j) for x, j in zip(nearer, late)]
    own_rows = [own] + arrived
    reduced = pl.pallas_call(
        functools.partial(z_sum_kernel, order[-1:] + order[:-1]),
        in_specs=[VMEM] * n_z,
        out_specs=VMEM,
        out_shape=block,
        scratch_shapes=[pltpu.VMEM((n_z, 8, cols), F32)],
        compiler_params=room(4),
        name="z_sum",
    )(*own_rows)
    final = [reduced] + [swap_region(reduced, i) for i in range(1, n_region)]
    hidden_grad, out_grad, loss = pl.pallas_call(
        finish_kernel,
        in_specs=[VMEM] * n_region,
        out_specs=[VMEM] * 3,
        out_shape=[
            jax.ShapeDtypeStruct((rows, hidden), F32),
            jax.ShapeDtypeStruct((1, hidden), F32),
            jax.ShapeDtypeStruct((1, 1), F32),
        ],
        scratch_shapes=[pltpu.VMEM((n_region, rows + TAIL, cols), BF)],
        compiler_params=room(4),
        name="finish",
    )(*final)
    return (hidden_grad, out_grad.reshape(hidden), loss.reshape(()))


def solution(mesh):
    return jax.shard_map(
        shards,
        mesh=mesh,
        in_specs=(
            P(("region", "shard"), None),
            P(("region", "shard")),
            P(("region", "shard"), None),
            P(("region", "shard")),
            P(("region", "shard"), None),
            P("shard", None),
            P("shard", None),
            P("shard", None),
            P(),
        ),
        out_specs=(P("shard", None), P(), P()),
        check_vma=False,
    )
```

```python
import functools

import jax
import jax.numpy as jnp
from jax import lax
from jax.experimental import pallas as pl
from jax.experimental.pallas import tpu as pltpu
from jax.sharding import PartitionSpec as P

BF = jnp.bfloat16
F32 = jnp.float32
REACH = 2
TAIL = 16
MIB = 1024 * 1024
VMEM = pl.BlockSpec(memory_space=pltpu.VMEM)


def along_z(array, by):
    devices = lax.axis_size("shard")
    return lax.ppermute(array, "shard", [(i, i ^ (2 * by)) for i in range(devices)])


def next_steps(n_z):
    return [j for j in range(1, n_z) if j & (j + 1) == 0]


def swap_core(array):
    devices = lax.axis_size("shard")
    return lax.ppermute(array, "shard", [(i, i ^ 1) for i in range(devices)])


def swap_region(array, by):
    devices = lax.axis_size("region")
    return lax.ppermute(array, "region", [(i, i ^ by) for i in range(devices)])


def room(mib):
    return pltpu.CompilerParams(vmem_limit_bytes=int(mib * MIB))


def identity(n):
    same = lax.broadcasted_iota(jnp.int32, (n, n), 0) == lax.broadcasted_iota(jnp.int32, (n, n), 1)
    return jnp.where(same, 1.0, 0.0).astype(BF)


def turned(one, array):
    return lax.dot_general(one, array, (((1,), (1,)), ((), ())), preferred_element_type=F32).astype(BF)


def split(value):
    high = value.astype(BF)
    return high, (value - high.astype(F32)).astype(BF)


def pack_tail(sums):
    high, low = split(sums)
    return jnp.concatenate([high.astype(F32), low.astype(F32)], axis=0).astype(BF)


def unpack_tail(rows):
    wide = rows.astype(F32)
    return wide[:8] + wide[8:]


def unit_rows(shard_at, rows, cols, region):
    first = shard_at * rows
    return pl.ds(pl.multiple_of(((first // cols) ^ region) * cols + first % cols, rows), rows)


def score_kernel(n_region, n_z, blk, *refs):
    half = 2 + n_region
    mine, other, rest = refs[:half], refs[half : 2 * half], refs[2 * half :]
    w_out, first_out, act_out, score_out, win_out, feat, own, w_in, w_mid, w_mid_t, anchors, dests = rest
    step = pl.program_id(0)
    region = lax.axis_index("region")
    shard = lax.axis_index("shard")
    z, core = shard // 2, shard % 2
    window = (2 * REACH + 1) * blk
    hidden, cols = w_mid.shape
    parts = feat.shape[1] // cols

    @pl.when(step == 0)
    def assemble():
        raw_cut = mine[0].shape[1] // 2
        dest_rows = (n_z - 1) * raw_cut
        steps = next_steps(n_z)
        feat_rows = (1 + len(steps)) * parts * blk
        slot_row = dest_rows + feat_rows
        slot_rows = -(-window // cols) * blk
        anchor_base = slot_row + slot_rows
        for source, core_at in ((mine, core), (other, 1 - core)):
            raw, mids, planes = source[0], source[1], source[2:]
            rows_mid = hidden // (2 * n_z)
            for j in range(n_z):
                shard_at = 2 * (z ^ j) + core_at
                at = pl.ds(pl.multiple_of(shard_at * raw_cut, raw_cut), raw_cut)
                mid = rows_mid + (n_z - 1 - j) * (rows_mid + raw_cut) if j > 0 else 0
                w_mid[unit_rows(shard_at, rows_mid, cols, z), :] = mids[mid : mid + rows_mid, :]
                for i in range(n_region):
                    base = (j - 1) * raw_cut
                    if j == 0:
                        w_in[i, at, :cols] = raw[i, :raw_cut, :]
                        w_in[i, at, cols:] = raw[i, raw_cut:, :]
                    else:
                        if i == n_region - 1:
                            w_in[i, at, :cols] = mids[mid + rows_mid : mid + rows_mid + raw_cut, :]
                        else:
                            w_in[i, at, :cols] = planes[i][anchor_base + base : anchor_base + base + raw_cut, :]
                        w_in[i, at, cols:] = planes[i][base : base + raw_cut, :]
        one = identity(cols)
        w_mid_t[...] = turned(one, w_mid[...])
        below_at = sum(jnp.where((z ^ (z - 1)) >= j, 1, 0) for j in steps)
        above_at = sum(jnp.where((z ^ (z + 1)) >= j, 1, 0) for j in steps)
        for i in range(n_region):
            near, far = mine[2 + i], other[2 + i]
            for t in range(parts):
                below, here, above = (
                    pl.ds(pl.multiple_of(dest_rows + (k * parts + t) * blk, blk), blk) for k in (below_at, 0, above_at)
                )
                lanes = slice(t * cols, (t + 1) * cols)
                before = jnp.where(core == 0, far[below, :], far[here, :])
                after = jnp.where(core == 0, far[here, :], far[above, :])
                for k, part in enumerate((near[below, :], before, near[here, :], after, near[above, :])):
                    feat[i * window + k * blk : i * window + (k + 1) * blk, lanes] = part
                own[i * blk : (i + 1) * blk, lanes] = near[here, :]
            spans = [
                near[slot_row + at : slot_row + at + blk, : min(cols, window - at // blk * cols)].astype(F32)
                for at in range(0, slot_rows, blk)
            ]
            win_out[i] = jnp.concatenate(spans + [jnp.zeros((blk, 128 - window), F32)], axis=1)
        for i in range(n_region):
            at = region ^ i ^ z
            dests[at] = jnp.dot(feat[...], w_in[i, :, cols:], preferred_element_type=F32)
            anchors[at] = jnp.dot(own[...], w_in[i, :, :cols], preferred_element_type=F32)

    group = 16
    pairs = group * window
    weight = w_out[...]
    for n in range(first_out.shape[0] // (blk * window)):
        reach_at = pl.ds(pl.multiple_of((step + n) * window, window), window)
        own_at = pl.ds(pl.multiple_of((step + n) * blk, blk), blk)
        for c in range(0, blk, group):
            base = (n * blk + c) * window
            for k in range(n_region):
                dest = dests[k, reach_at, :]
                line = anchors[k, own_at, :]
                for a in range(group):
                    total = dest + line[c + a : c + a + 1, :]
                    at = slice(base + a * window, base + (a + 1) * window)
                    first_out[at, k * cols : (k + 1) * cols] = jnp.maximum(total.astype(BF), 0)
            second = lax.dot_general(
                w_mid_t[...], first_out[base : base + pairs, :], (((1,), (1,)), ((), ())), preferred_element_type=F32
            )
            active = jnp.maximum(second, 0.0)
            act_out[:, base : base + pairs] = active.astype(BF)
            score = jnp.sum(active * weight, axis=0, keepdims=True)
            for a in range(group):
                row = n * blk + c + a
                score_out[row : row + 1, :] = jnp.concatenate(
                    [score[:, a * window : (a + 1) * window], jnp.zeros((1, 128 - window), F32)], axis=1
                )


def add_targets(grad, pre, first, targets, width):
    for n, j in enumerate(targets):
        grad[n] += jnp.dot(pre[...], first[:, j * width : (j + 1) * width], preferred_element_type=F32)


def put_blocks(grad, turn, tail, keep, send):
    rows = keep.shape[1] - TAIL
    core = lax.axis_index("shard") % 2
    for n in range(keep.shape[0]):
        turn[n] = grad[n].T
        for target, core_at in ((keep, core), (send, 1 - core)):
            target[n, :rows, :] = turn[n, pl.ds(pl.multiple_of(core_at * rows, rows), rows), :].astype(BF)
            target[n, rows:, :] = tail


def rest_kernel(targets, *refs):
    first, pre, tail, keep, send, grad, turn = refs

    @pl.when(pl.program_id(0) == 0)
    def clear():
        grad[...] = jnp.zeros_like(grad)

    add_targets(grad, pre, first, targets, grad.shape[2])

    @pl.when(pl.program_id(0) == pl.num_programs(0) - 1)
    def finish():
        put_blocks(grad, turn, tail[...], keep, send)


def grad_kernel(n_region, targets, window, *refs):
    scores, rest = refs[:n_region], refs[n_region:]
    win, first, act, w_out, pre_out, tail_out, keep, send, grad, turn, gout, sums = rest
    step = pl.program_id(0)
    cols = act.shape[0]
    blk = win.shape[1]

    @pl.when(step == 0)
    def clear():
        grad[...] = jnp.zeros_like(grad)
        gout[...] = jnp.zeros_like(gout)
        sums[...] = jnp.zeros_like(sums)

    weight = jnp.broadcast_to(w_out[...], (cols, 128))
    gained = gout[...]
    trips, numer = sums[0], sums[1]
    group = 8
    regions = act.shape[1] // (blk * window)
    score = scores[0][...]
    for k in range(1, n_region):
        order = [n ^ k if regions > 1 else 0 for n in range(regions)]
        score = score + jnp.concatenate([scores[k][n * blk : (n + 1) * blk, :] for n in order], axis=0)
    table = jnp.concatenate([win[step + n] for n in range(regions)], axis=0)
    valid = table > 0
    flow = jnp.where(valid, table - 1.0, 0.0)
    top = jnp.max(jnp.where(valid, score, -jnp.inf), axis=1, keepdims=True)
    expo = jnp.where(valid, jnp.exp(score - top), 0.0)
    mass = jnp.sum(expo, axis=1, keepdims=True)
    probs = expo / mass
    logp = score - top - jnp.log(mass)
    anchor_total = jnp.sum(flow, axis=1, keepdims=True)
    sgrad = jnp.where(valid, probs * anchor_total - flow, 0.0)
    lost = jnp.where(valid, flow * logp, 0.0)
    for n in range(regions):
        trips = trips + flow[n * blk : (n + 1) * blk, :]
        numer = numer - lost[n * blk : (n + 1) * blk, :]
    for c in range(0, regions * blk, group):
        wide = jnp.concatenate([sgrad[c + a : c + a + 1, :window] for a in range(group)], axis=1)
        for q in range(0, group * window, 128):
            line = wide[:, q : q + 128]
            at = slice(c * window + q, c * window + q + 128)
            active = act[:, at].astype(F32)
            gained = gained + active * line
            pre_out[:, at] = jnp.where(active > 0, weight * line, 0.0).astype(BF)
    gout[...] = gained
    sums[0] = trips
    sums[1] = numer
    add_targets(grad, pre_out, first, targets, grad.shape[2])

    @pl.when(step == pl.num_programs(0) - 1)
    def finish():
        out = jnp.sum(gout[...].T, axis=0, keepdims=True)
        total = jnp.sum(sums[0])
        numer = jnp.sum(sums[1])
        row = lax.broadcasted_iota(jnp.int32, (8, cols), 0)
        lane = lax.broadcasted_iota(jnp.int32, (8, cols), 1)
        stats = jnp.where(lane == 0, total, jnp.where(lane == 1, numer, 0.0))
        tail = pack_tail(jnp.where(row == 0, out, jnp.where(row == 1, stats, 0.0)))
        tail_out[...] = tail
        put_blocks(grad, turn, tail, keep, send)


def core_sum_kernel(keep, received, *outs):
    for j, out in enumerate(outs):
        rows = out.shape[0] - TAIL
        out[:rows, :] = (keep[j, :rows, :].astype(F32) + received[j, :rows, :].astype(F32)).astype(BF)
        out[rows:, :] = pack_tail(unpack_tail(keep[j, rows:, :]) + unpack_tail(received[j, rows:, :]))


def z_sum_kernel(steps, *refs):
    blocks, (out, tails) = refs[:-2], refs[-2:]
    n_z = len(blocks)
    rows = out.shape[0] - TAIL
    total = blocks[0][:rows, :].astype(F32)
    for block in blocks[1:]:
        total = total + block[:rows, :].astype(F32)
    out[:rows, :] = total.astype(BF)
    for j, block in zip(steps, blocks):
        tails[j] = unpack_tail(block[rows:, :])
    z = lax.axis_index("shard") // 2
    tail = tails[z]
    for z_at in range(1, n_z):
        tail = tail + tails[z ^ z_at]
    out[rows:, :] = pack_tail(tail)


def finish_kernel(*refs):
    blocks, (grad, out_grad, loss, held) = refs[:-4], refs[-4:]
    n_region = len(blocks)
    cols = blocks[0].shape[1]
    rows = grad.shape[0]
    for i, block in enumerate(blocks):
        held[i] = block[...]
    region = lax.axis_index("region")
    stats = unpack_tail(held[region][rows:, :])
    total = stats[1:2, 0:1]
    numer = stats[1:2, 1:2]
    loss[...] = numer / total
    inverse = 1.0 / total
    for q in range(n_region):
        block = held[region ^ q]
        grad[:, q * cols : (q + 1) * cols] = block[:rows, :].astype(F32) * inverse
        out_grad[:, q * cols : (q + 1) * cols] = unpack_tail(block[rows:, :])[0:1, :] * inverse


def shards(tiles, tile_block, neighbors, counts, flows, w_anchor, w_dest, w_hidden, w_out):
    blk = counts.shape[0]
    slots = neighbors.shape[1]
    n_region = lax.axis_size("region")
    n_shard = lax.axis_size("shard")
    n_z = n_shard // 2
    hidden = w_hidden.shape[1]
    rows_in = w_anchor.shape[0]
    depth = rows_in * n_shard
    cols = hidden // n_region
    window = (2 * REACH + 1) * blk
    pairs = blk * window
    region = lax.axis_index("region")

    def cut(array, i):
        return lax.dynamic_slice_in_dim(array, (region ^ i) * cols, cols, array.ndim - 1)

    def along_rows(features):
        return [features[:, t * cols : (t + 1) * cols] for t in range(depth // cols)]

    piece = jnp.concatenate([cut(w_anchor, 0), cut(w_dest, 0)], axis=0)

    piece, tile_block = lax.optimization_barrier((piece, tile_block))
    onehot = (tile_block[None, :] == jnp.arange(blk, dtype=jnp.int32)[:, None]).astype(BF)
    sums = jnp.dot(onehot, tiles, preferred_element_type=F32)
    scale = lax.rsqrt(jnp.mean(sums * sums, axis=-1, keepdims=True) + 1e-05)
    features = jnp.concatenate(along_rows((sums * scale).astype(BF)), axis=0)

    payload = jnp.concatenate([piece, features], axis=0)
    from_z = [along_z(payload if j in next_steps(n_z) else piece, j) for j in range(1, n_z)]
    w_anchor, w_dest, payload = lax.optimization_barrier((w_anchor, w_dest, payload))
    raw = jnp.stack([jnp.concatenate([cut(w_anchor, i), cut(w_dest, i)], axis=0) for i in range(n_region)])

    spot = neighbors % (blk * n_shard) - (lax.axis_index("shard") - REACH) * blk
    valid = jnp.arange(slots, dtype=jnp.int32)[None, :] < counts[:, None]
    held_by = (spot[:, :, None] == jnp.arange(window, dtype=jnp.int32)) & valid[:, :, None]
    slot_table = jnp.sum(jnp.where(held_by, flows[:, :, None] + 1, 0), axis=1).astype(BF)
    slot_table = jnp.pad(slot_table, ((0, 0), (0, -window % cols)))
    slot_table = jnp.concatenate([slot_table[:, k : k + cols] for k in range(0, slot_table.shape[1], cols)], axis=0)

    held = 2 * rows_in
    around = [features] + [from_z[j - 1][held:] for j in next_steps(n_z)]
    shared = jnp.concatenate([p[rows_in:held] for p in from_z] + around + [slot_table], axis=0)
    plane = jnp.concatenate([shared] + [p[:rows_in] for p in from_z], axis=0)
    planes = [plane] + [swap_region(plane, i) for i in range(1, n_region - 1)] + [swap_region(shared, n_region - 1)]

    mid_raw = cut(w_hidden, 0)
    far_plane = swap_core(plane)
    mid_send, far_plane = lax.optimization_barrier(
        (jnp.concatenate([mid_raw, cut(w_anchor, n_region - 1)], axis=0), far_plane)
    )
    mids = jnp.concatenate([mid_raw] + [along_z(mid_send, j) for j in range(1, n_z)][::-1], axis=0)
    mine = [raw, mids, *planes]
    other = [swap_core(raw), swap_core(mids), far_plane] + [swap_core(x) for x in planes[1:]]
    weight_out = cut(w_out, 0).astype(F32).reshape(cols, 1)

    resident = 2 * hidden * n_region * pairs <= 12 * MIB

    steps = 1 if resident else n_region
    by_anchors = VMEM if resident else pl.BlockSpec((blk, 128), lambda i: (i, 0))

    def by_pairs(rows):
        return VMEM if resident else pl.BlockSpec((rows, pairs), lambda i: (0, i))

    pair_rows = VMEM if resident else pl.BlockSpec((pairs, hidden), lambda i: (i, 0))

    first, act, score, win = pl.pallas_call(
        functools.partial(score_kernel, n_region, n_z, blk),
        grid=(steps,),
        in_specs=[VMEM] * (2 * len(mine) + 1),
        out_specs=[pair_rows, by_pairs(cols), by_anchors, VMEM],
        scratch_shapes=[
            pltpu.VMEM((n_region * window, depth), BF),
            pltpu.VMEM((n_region * blk, depth), BF),
            pltpu.VMEM((n_region, depth, 2 * cols), BF),
            pltpu.VMEM((hidden, cols), BF),
            pltpu.VMEM((cols, hidden), BF),
            pltpu.VMEM((n_region, n_region * blk, cols), F32),
            pltpu.VMEM((n_region, n_region * window, cols), F32),
        ],
        out_shape=[
            jax.ShapeDtypeStruct((n_region * pairs, hidden), BF),
            jax.ShapeDtypeStruct((cols, n_region * pairs), BF),
            jax.ShapeDtypeStruct((n_region * blk, 128), F32),
            jax.ShapeDtypeStruct((n_region, blk, 128), F32),
        ],
        compiler_params=room(14 + 1.25 * n_region),
        name="scores",
    )(*mine, *other, weight_out)

    parts = [score] + [swap_region(score, i) for i in range(1, n_region)]
    rows = hidden // n_shard
    block = jax.ShapeDtypeStruct((rows + TAIL, cols), BF)
    order = list(range(n_z))[::-1]
    early, late = order[: n_z // 2], order[n_z // 2 :]

    def blocks(targets):
        return jax.ShapeDtypeStruct((len(targets), rows + TAIL, cols), BF)

    def core_sum(keep, received):
        return pl.pallas_call(
            core_sum_kernel,
            in_specs=[VMEM] * 2,
            out_specs=[VMEM] * keep.shape[0],
            out_shape=[block] * keep.shape[0],
            compiler_params=room(4),
            name="core_sum",
        )(keep, received)

    def turns(targets):
        return [pltpu.VMEM((len(targets), *x), F32) for x in ((cols, 2 * rows), (2 * rows, cols))]

    def rest(targets, pre):
        return pl.pallas_call(
            functools.partial(rest_kernel, targets),
            grid=(steps,),
            in_specs=[pair_rows, by_pairs(cols), VMEM],
            out_specs=[VMEM] * 2,
            scratch_shapes=turns(targets),
            out_shape=[blocks(targets)] * 2,
            compiler_params=room(14),
            name="gradient_rest",
        )(first, pre, tail)

    pre, tail, keep, send = pl.pallas_call(
        functools.partial(grad_kernel, n_region, early, window),
        grid=(steps,),
        in_specs=[
            VMEM if resident else pl.BlockSpec((blk, 128), functools.partial(lambda k, i: (i ^ k, 0), k))
            for k in range(n_region)
        ]
        + [VMEM, pair_rows, by_pairs(cols), VMEM],
        out_specs=[by_pairs(cols)] + [VMEM] * 3,
        scratch_shapes=turns(early) + [pltpu.VMEM((cols, 128), F32), pltpu.VMEM((2, blk, 128), F32)],
        out_shape=[
            jax.ShapeDtypeStruct((cols, n_region * pairs), BF),
            jax.ShapeDtypeStruct((TAIL, cols), BF),
            blocks(early),
            blocks(early),
        ],
        compiler_params=room(14),
        name="gradient",
    )(*parts, win, first, act, weight_out)
    received = swap_core(send)
    keep_late, send_late = rest(late, pre)
    received, keep_late, send_late = lax.optimization_barrier((received, keep_late, send_late))
    sums = core_sum(keep, received)
    arrived = [along_z(x, j) for x, j in zip(sums, early)]
    *nearer, own = core_sum(keep_late, swap_core(send_late))
    arrived += [along_z(x, j) for x, j in zip(nearer, late)]
    own_rows = [own] + arrived
    reduced = pl.pallas_call(
        functools.partial(z_sum_kernel, order[-1:] + order[:-1]),
        in_specs=[VMEM] * n_z,
        out_specs=VMEM,
        out_shape=block,
        scratch_shapes=[pltpu.VMEM((n_z, 8, cols), F32)],
        compiler_params=room(4),
        name="z_sum",
    )(*own_rows)
    final = [reduced] + [swap_region(reduced, i) for i in range(1, n_region)]
    hidden_grad, out_grad, loss = pl.pallas_call(
        finish_kernel,
        in_specs=[VMEM] * n_region,
        out_specs=[VMEM] * 3,
        out_shape=[
            jax.ShapeDtypeStruct((rows, hidden), F32),
            jax.ShapeDtypeStruct((1, hidden), F32),
            jax.ShapeDtypeStruct((1, 1), F32),
        ],
        scratch_shapes=[pltpu.VMEM((n_region, rows + TAIL, cols), BF)],
        compiler_params=room(4),
        name="finish",
    )(*final)
    return (hidden_grad, out_grad.reshape(hidden), loss.reshape(()))


def solution(mesh):
    return jax.shard_map(
        shards,
        mesh=mesh,
        in_specs=(
            P(("region", "shard"), None),
            P(("region", "shard")),
            P(("region", "shard"), None),
            P(("region", "shard")),
            P(("region", "shard"), None),
            P("shard", None),
            P("shard", None),
            P("shard", None),
            P(),
        ),
        out_specs=(P("shard", None), P(), P()),
        check_vma=False,
    )
```
